32 devices in a mesh: batch: 8 (over y, x, core), latent: 4 (over z).
Axes of the slice: x: 2, y: 2, z: 4, core: 2. Of those that a mesh axis runs over, the one named last changes fastest.
Arguments:
- rows: bfloat16 [4096, 2048], P('batch', 'latent'), may hold values from -8 to 8, as said below
- targets: bfloat16 [256, 2048], P('batch', 'latent'), may hold values from -16 to 16
- w_up: bfloat16 [2048, 1024], P('latent'), may hold values from -2.5 to 2.5
- bias: float32 [1024], replicated, may hold values from -3 to 3
- history: int32 [256, 512], P('batch'), may hold values from 0 to 511, as said below
- requests: int32 [64, 64], P('batch'), may hold values from -1 to 511, as said below
- upstream: bfloat16 [256, 1024], P('batch', 'latent'), may hold values from -6 to 6
Outputs:
- output: bfloat16 [256, 1024], P('batch', 'latent')
- row_grad: float32 [4096, 2048], P('batch', 'latent')
The draws below stay inside these ranges and needn't reach their ends.
Inputs may be any that keep to these rules, and one draw needn't show every extreme that they name: `requests`: row d * 8 + o lists distinct owner-local row numbers in its first entries and -1 after them, with at least one live entry; for the last owner and for one owner drawn anew, every list is full. `history`: every entry names a live slot of its user's device. `rows`: values of order one.
All inputs are finite; a program needn't handle non-finite values.
Results may differ from the reference program's by a relative error of at most 0.012.
The reference program's roundings to bfloat16 on the way count: a program that leaves them out, or rounds other values in their place, can miss the bound.
Values may be sent and summed in bfloat16 or wider, within the bound.
No kernel may reach another device: no remote copies, remote signals or barrier semaphores. Data moves between devices by JAX's collectives and lax.ppermute only.
A program may use at most 64 MiB of HBM per device.

```python
import jax
import jax.numpy as jnp
from jax import lax

DL = 2048
H = 1024
HIST = 512
CAP = 64
USERS_DEV = 32
ROWS_DEV = 512
OWNERS = 8
USERS = 256
SLOTS = 512
ROWS = 4096


def shared_routes(key):
    base = jax.random.fold_in(key, 11)
    counts = jax.random.randint(jax.random.fold_in(base, 1), (OWNERS, OWNERS), max(CAP // 4, 1), CAP + 1)
    hottest = jax.random.randint(jax.random.fold_in(base, 2), (), 0, OWNERS)
    owner_ids = jnp.arange(OWNERS)[None, :]
    counts = jnp.where((owner_ids == hottest) | (owner_ids == OWNERS - 1), CAP, counts)
    ranking = jax.random.randint(jax.random.fold_in(base, 3), (OWNERS * OWNERS, ROWS_DEV), 0, 65536)
    ranking = ranking * ROWS_DEV + jnp.arange(ROWS_DEV, dtype=jnp.int32)[None, :]
    ordered = jnp.argsort(ranking, axis=1)[:, :CAP].astype(jnp.int32)
    living = jnp.arange(CAP)[None, :] < counts.reshape(-1)[:, None]
    requests = jnp.where(living, ordered, -1).astype(jnp.int32)
    device = jnp.arange(USERS, dtype=jnp.int32) // USERS_DEV
    owner_pick = jax.random.randint(jax.random.fold_in(base, 4), (USERS, HIST), 0, OWNERS)
    limits = counts[device[:, None], owner_pick]
    entries = jax.random.randint(jax.random.fold_in(base, 5), (USERS, HIST), 0, 1048576) % limits
    history = (owner_pick * CAP + entries).astype(jnp.int32)
    history = history.at[0, HIST - 1].set(SLOTS - 1)
    history = history.at[0, HIST - 2].set(0)
    return (requests, history.astype(jnp.int32))


def shared_floats(key):
    base = jax.random.fold_in(key, 31)
    rows = jnp.clip(jax.random.normal(jax.random.fold_in(base, 8), (ROWS, DL)), -4.0, 4.0)
    targets = jnp.clip(jax.random.normal(jax.random.fold_in(base, 9), (USERS, DL)), -4.0, 4.0)
    return (rows.astype(jnp.float32), targets.astype(jnp.float32))


def draw_requests(key, part):
    return shared_routes(key)[0]


def draw_history(key, part):
    return shared_routes(key)[1]


def draw_rows(key, part):
    return shared_floats(key)[0].astype(jnp.bfloat16)


def draw_targets(key, part):
    return shared_floats(key)[1].astype(jnp.bfloat16)


def shard_levels(stream_key, extent, shards, smallest, top_value):
    def one(position, shards_of):
        draws = jax.random.uniform(jax.random.fold_in(jax.random.fold_in(stream_key, 6), position), (shards_of,), jnp.float32, smallest / len(shards), top_value / len(shards))
        return jnp.repeat(jnp.exp(draws), extent[position] // shards_of).reshape((-1,) + (1,) * (len(extent) - position - 1))

    gain = one(*shards[0])
    for cut in shards[1:]:
        gain = gain * one(*cut)
    return gain


def scatter_about(own_key, shape, width, most, split=(), held_as=jnp.bfloat16):
    values = width * jax.random.normal(own_key, shape, jnp.float32)
    if split:
        values = values * shard_levels(own_key, shape, split, -0.22, 0.18)
    return jnp.clip(values, -most, most).astype(held_as)


def setup_inputs(seed: int = 0) -> dict:
    key_list = jax.random.split(jax.random.key(seed), 8)
    return {
        "rows": draw_rows(jax.random.fold_in(key_list[7], 71), 0),
        "targets": draw_targets(jax.random.fold_in(key_list[7], 71), 0),
        "w_up": scatter_about(key_list[2], (DL, H), (max(DL // 400, 1)) ** -0.5, 2.5, ((0, 4),)),
        "bias": scatter_about(key_list[3], (H,), 0.5, 3.0, (), jnp.float32),
        "history": draw_history(jax.random.fold_in(key_list[7], 71), 0),
        "requests": draw_requests(jax.random.fold_in(key_list[7], 71), 0),
        "upstream": scatter_about(key_list[6], (USERS, H), 1.0, 6.0, ((0, 8), (1, 4))),
    }


def reference(rows, targets, w_up, bias, history, requests, upstream):
    score_scale = DL ** (-0.5)
    listed = requests.reshape(OWNERS, OWNERS, CAP)
    base_rows = (jnp.arange(OWNERS, dtype=jnp.int32) * ROWS_DEV)[None, :, None]
    slot_row = jnp.where(listed >= 0, base_rows + listed, ROWS).reshape(OWNERS, SLOTS).astype(jnp.int32)
    padded = jnp.concatenate([rows, jnp.zeros((1, DL), rows.dtype)], axis=0)
    queries = targets.reshape(OWNERS, USERS_DEV, DL)
    picks = history.reshape(OWNERS, USERS_DEV, HIST)
    upper = upstream.reshape(OWNERS, USERS_DEV, H)
    flat_users = (jnp.arange(USERS_DEV, dtype=jnp.int32) * SLOTS)[:, None]

    def device_step(summed, inputs):
        slot_rows, query_rows, history_rows, upstream_rows = inputs
        fetched = padded[slot_rows]
        slot_scores = jnp.dot(query_rows, fetched.T, preferred_element_type=jnp.float32)
        scores = jnp.take_along_axis(slot_scores, history_rows, axis=1) * score_scale
        probability = jax.nn.softmax(scores, axis=1)
        segment_ids = (history_rows + flat_users).reshape(-1).astype(jnp.int32)
        weight = jax.ops.segment_sum(probability.reshape(-1), segment_ids, USERS_DEV * SLOTS).reshape(USERS_DEV, SLOTS)
        pooled = jnp.dot(weight.astype(jnp.bfloat16), fetched, preferred_element_type=jnp.float32).astype(jnp.bfloat16)
        hidden = jnp.dot(pooled, w_up, preferred_element_type=jnp.float32) + bias
        activated, backward = jax.vjp(jax.nn.gelu, hidden)
        slopes = backward(upstream_rows.astype(jnp.float32))[0].astype(jnp.bfloat16)
        pooled_grad = jnp.dot(slopes, w_up.T, preferred_element_type=jnp.float32)
        slot_slopes = jnp.dot(pooled_grad.astype(jnp.bfloat16), fetched.T, preferred_element_type=jnp.float32)
        probability_grad = jnp.take_along_axis(slot_slopes, history_rows, axis=1)
        score_grad = probability * (probability_grad - lax.optimization_barrier(jnp.sum(probability * probability_grad, axis=1, keepdims=True)))
        weight_grad = jax.ops.segment_sum(score_grad.reshape(-1), segment_ids, USERS_DEV * SLOTS).reshape(USERS_DEV, SLOTS)
        slot_grad = jnp.dot(weight.T, pooled_grad, precision=lax.Precision.HIGHEST)
        slot_grad = slot_grad + score_scale * jnp.dot(weight_grad.T, query_rows.astype(jnp.float32), precision=lax.Precision.HIGHEST)
        summed = summed + jax.ops.segment_sum(slot_grad, slot_rows, ROWS + 1)
        return (summed, activated.astype(jnp.bfloat16))
    summed, outputs = lax.scan(device_step, jnp.zeros((ROWS + 1, DL), jnp.float32), (slot_row, queries, picks, upper))
    return (outputs.reshape(USERS, H), summed[:ROWS])
```

```python
import jax
import jax.numpy as jnp
from jax import lax
from jax.sharding import PartitionSpec as P

DL = 2048


def swap(x, axis, k):
    n = lax.axis_size(axis)
    return lax.ppermute(x, axis, [(i, i ^ k) for i in range(n)])


def sum_all(x, axis):
    n = lax.axis_size(axis)
    parts = [swap(x, axis, k) for k in range(1, n)]
    for part in parts:
        x = x + part
    return x


def sum_share(x, axis):
    n = lax.axis_size(axis)
    me = lax.axis_index(axis)
    width = x.shape[1] // n

    def share(k):
        return lax.dynamic_slice_in_dim(x, (me ^ k) * width, width, axis=1)

    parts = [swap(share(k), axis, k) for k in range(1, n)]
    total = share(0)
    for part in parts:
        total = total + part
    return total


def gather_columns(x, axis):
    n = lax.axis_size(axis)
    me = lax.axis_index(axis)
    parts = jnp.stack([x] + [swap(x, axis, k) for k in range(1, n)])
    ordered = [lax.dynamic_index_in_dim(parts, me ^ i, 0, keepdims=False) for i in range(n)]
    return jnp.concatenate(ordered, axis=1)


def exchange(x):
    return lax.all_to_all(x, "batch", split_axis=0, concat_axis=0, tiled=True)


def on_device(rows, targets, w_up, bias, history, requests, upstream):
    score_scale = DL ** (-0.5)
    owners = lax.axis_size("batch")
    capacity = requests.shape[1]
    slot_count = owners * capacity
    row_width = rows.shape[1]
    stored = rows.shape[0]
    hidden_share = upstream.shape[1]

    wanted = exchange(requests).reshape(-1)
    places = lax.broadcasted_iota(jnp.int32, (slot_count, stored), 1)
    chosen = jnp.dot(
        (wanted[:, None] == places).astype(jnp.bfloat16), rows, preferred_element_type=jnp.float32
    ).astype(jnp.bfloat16)
    fetched = exchange(chosen.reshape(owners, capacity, row_width)).reshape(slot_count, row_width)

    slots = lax.broadcasted_iota(jnp.int32, (1, 1, slot_count), 2)
    count = jnp.sum((history[:, :, None] == slots).astype(jnp.float32), axis=1)

    slot_scores = jnp.einsum("ud,sd->us", targets, fetched, preferred_element_type=jnp.float32)
    scores = sum_all(slot_scores, "latent") * score_scale
    top = jnp.max(jnp.where(count > 0, scores, -jnp.inf), axis=1, keepdims=True)
    raised = jnp.where(count > 0, count * jnp.exp(scores - top), 0.0)
    weight = raised / jnp.sum(raised, axis=1, keepdims=True)

    pooled = jnp.dot(
        weight.astype(jnp.bfloat16), fetched, preferred_element_type=jnp.float32
    ).astype(jnp.bfloat16)
    partial_hidden = jnp.dot(pooled, w_up, preferred_element_type=jnp.float32)
    column = lax.axis_index("latent") * hidden_share
    hidden = sum_share(partial_hidden, "latent")
    hidden = hidden + lax.dynamic_slice_in_dim(bias, column, hidden_share)
    activated, backward = jax.vjp(jax.nn.gelu, hidden)
    output = activated.astype(jnp.bfloat16)
    slopes = backward(upstream.astype(jnp.float32))[0].astype(jnp.bfloat16)
    slopes_full = gather_columns(slopes, "latent")
    pooled_grad = jnp.einsum("uh,dh->ud", slopes_full, w_up, preferred_element_type=jnp.float32)
    slot_slopes = jnp.einsum(
        "ud,sd->us", pooled_grad.astype(jnp.bfloat16), fetched, preferred_element_type=jnp.float32
    )
    whole_slopes = sum_all(slot_slopes, "latent")
    weight_grad = weight * (
        whole_slopes - jnp.sum(weight * whole_slopes, axis=1, keepdims=True)
    )
    slot_grad = jnp.einsum("us,ud->sd", weight, pooled_grad, precision=lax.Precision.HIGHEST)
    slot_grad = slot_grad + score_scale * jnp.einsum(
        "us,ud->sd", weight_grad, targets.astype(jnp.float32), precision=lax.Precision.HIGHEST
    )
    returned = exchange(
        slot_grad.astype(jnp.bfloat16).reshape(owners, capacity, row_width)
    ).reshape(slot_count, row_width)
    row_grad = jnp.dot(
        (places.T == wanted[None, :]).astype(jnp.bfloat16),
        returned,
        preferred_element_type=jnp.float32,
    )
    return (output, row_grad)


def solution(mesh):
    return jax.shard_map(
        on_device,
        mesh=mesh,
        in_specs=(
            P("batch", "latent"),
            P("batch", "latent"),
            P("latent", None),
            P(),
            P("batch", None),
            P("batch", None),
            P("batch", "latent"),
        ),
        out_specs=(P("batch", "latent"), P("batch", "latent")),
        check_vma=False,
    )
```

```python
import jax
import jax.numpy as jnp
from jax import lax
from jax.sharding import PartitionSpec as P

DL = 2048


def swap(x, axis, k):
    n = lax.axis_size(axis)
    return lax.ppermute(x, axis, [(i, i ^ k) for i in range(n)])


def sum_all(x, axis):
    n = lax.axis_size(axis)
    parts = [swap(x, axis, k) for k in range(1, n)]
    total = x.astype(jnp.float32)
    for part in parts:
        total = total + part.astype(jnp.float32)
    return total


def gather_columns(x, axis):
    n = lax.axis_size(axis)
    me = lax.axis_index(axis)
    parts = jnp.stack([x] + [swap(x, axis, k) for k in range(1, n)])
    ordered = [lax.dynamic_index_in_dim(parts, me ^ i, 0, keepdims=False) for i in range(n)]
    return jnp.concatenate(ordered, axis=1)


def exchange(x):
    return lax.all_to_all(x, "batch", split_axis=0, concat_axis=0, tiled=True)


def on_device(rows, targets, w_up, bias, history, requests, upstream):
    score_scale = DL ** (-0.5)
    owners = lax.axis_size("batch")
    capacity = requests.shape[1]
    slot_count = owners * capacity
    row_width = rows.shape[1]
    stored = rows.shape[0]
    hidden_share = upstream.shape[1]

    wanted = exchange(requests).reshape(-1)
    places = lax.broadcasted_iota(jnp.int32, (slot_count, stored), 1)
    chosen = jnp.dot(
        (wanted[:, None] == places).astype(jnp.bfloat16), rows, preferred_element_type=jnp.float32
    ).astype(jnp.bfloat16)
    fetched = exchange(chosen.reshape(owners, capacity, row_width)).reshape(slot_count, row_width)

    slots = lax.broadcasted_iota(jnp.int32, (1, 1, slot_count), 2)
    count = jnp.sum((history[:, :, None] == slots).astype(jnp.float32), axis=1)
    upstream_full = gather_columns(upstream, "latent")
    fetched, count, upstream_full = lax.optimization_barrier((fetched, count, upstream_full))

    slot_scores = jnp.einsum("ud,sd->us", targets, fetched, preferred_element_type=jnp.float32)
    scores = sum_all(slot_scores, "latent") * score_scale
    top = jnp.max(jnp.where(count > 0, scores, -jnp.inf), axis=1, keepdims=True)
    raised = jnp.where(count > 0, count * jnp.exp(scores - top), 0.0)
    weight = raised / jnp.sum(raised, axis=1, keepdims=True)

    pooled = jnp.dot(
        weight.astype(jnp.bfloat16), fetched, preferred_element_type=jnp.float32
    ).astype(jnp.bfloat16)
    partial_hidden = jnp.dot(pooled, w_up, preferred_element_type=jnp.float32)
    hidden = sum_all(partial_hidden.astype(jnp.bfloat16), "latent") + bias
    activated, backward = jax.vjp(jax.nn.gelu, hidden)
    column = lax.axis_index("latent") * hidden_share
    output = lax.dynamic_slice_in_dim(activated.astype(jnp.bfloat16), column, hidden_share, axis=1)
    slopes = backward(upstream_full.astype(jnp.float32))[0].astype(jnp.bfloat16)
    pooled_grad = jnp.einsum("uh,dh->ud", slopes, w_up, preferred_element_type=jnp.float32)
    slot_slopes = jnp.einsum(
        "ud,sd->us", pooled_grad.astype(jnp.bfloat16), fetched, preferred_element_type=jnp.float32
    )
    whole_slopes = sum_all(slot_slopes, "latent")
    weight_grad = weight * (
        whole_slopes - jnp.sum(weight * whole_slopes, axis=1, keepdims=True)
    )
    slot_grad = jnp.einsum("us,ud->sd", weight, pooled_grad, precision=lax.Precision.HIGHEST)
    slot_grad = slot_grad + score_scale * jnp.einsum(
        "us,ud->sd", weight_grad, targets.astype(jnp.float32), precision=lax.Precision.HIGHEST
    )
    returned = exchange(
        slot_grad.astype(jnp.bfloat16).reshape(owners, capacity, row_width)
    ).reshape(slot_count, row_width)
    row_grad = jnp.dot(
        (places.T == wanted[None, :]).astype(jnp.bfloat16),
        returned,
        preferred_element_type=jnp.float32,
    )
    return (output, row_grad)


def solution(mesh):
    return jax.shard_map(
        on_device,
        mesh=mesh,
        in_specs=(
            P("batch", "latent"),
            P("batch", "latent"),
            P("latent", None),
            P(),
            P("batch", None),
            P("batch", None),
            P("batch", "latent"),
        ),
        out_specs=(P("batch", "latent"), P("batch", "latent")),
        check_vma=False,
    )
```

```python
import functools

import jax
import jax.numpy as jnp
from jax import lax
from jax.experimental import pallas as pl
from jax.experimental.pallas import tpu as pltpu
from jax.sharding import PartitionSpec as P

DL = 2048


def swap(x, axis, k):
    n = lax.axis_size(axis)
    return lax.ppermute(x, axis, [(i, i ^ k) for i in range(n)])


def sum_all(x, axis):
    n = lax.axis_size(axis)
    parts = [swap(x, axis, k) for k in range(1, n)]
    total = x.astype(jnp.float32)
    for part in parts:
        total = total + part.astype(jnp.float32)
    return total


def gather_columns(x, axis):
    n = lax.axis_size(axis)
    me = lax.axis_index(axis)
    parts = jnp.stack([x] + [swap(x, axis, k) for k in range(1, n)])
    ordered = [lax.dynamic_index_in_dim(parts, me ^ i, 0, keepdims=False) for i in range(n)]
    return jnp.concatenate(ordered, axis=1)


def exchange(x):
    return lax.all_to_all(x, "batch", split_axis=0, concat_axis=0, tiled=True)


def gather_chips(x, axis):
    n = lax.axis_size(axis)
    return jnp.concatenate([x] + [swap(x, axis, k) for k in range(2, n, 2)], axis=0)


def pick_rows(wanted_ref, rows_ref, out_ref):
    owners, capacity = wanted_ref.shape[0], wanted_ref.shape[2]
    stored = rows_ref.shape[0]
    listed = wanted_ref[...].reshape(owners, capacity).T
    places = lax.broadcasted_iota(jnp.int32, (capacity, stored), 1)
    chosen = jnp.concatenate(
        [(listed[:, d : d + 1] == places).astype(jnp.bfloat16) for d in range(owners)], axis=0
    )
    out_ref[...] = jnp.dot(chosen, rows_ref[...], preferred_element_type=jnp.float32).astype(
        jnp.bfloat16
    )


def add_rows(
    latents,
    me_ref,
    wanted_ref,
    sent_ref,
    even_targets_ref,
    odd_targets_ref,
    even_grads_ref,
    odd_grads_ref,
    out_ref,
    left_ref,
    right_ref,
):
    owners, capacity = wanted_ref.shape[0], wanted_ref.shape[2]
    stored = out_ref.shape[0]
    members = even_grads_ref.shape[0] // (owners // 2)
    half = members // 2
    share = half // latents
    places = lax.broadcasted_iota(jnp.int32, (stored, capacity), 0)
    me = me_ref[0]

    def unpack(x):
        return jnp.concatenate([x[:, :capacity], x[:, capacity:]], axis=0)

    for k in range(owners):
        d = me ^ k
        block = sent_ref[pl.ds(d * latents, latents)]
        slope = block[0, :half]
        for z in range(1, latents):
            slope = slope + block[z, :half]
        weight = jnp.concatenate([block[z, half : half + share] for z in range(latents)], axis=0)
        factor = jnp.concatenate([unpack(weight), unpack(slope)], axis=0)
        high = factor.astype(jnp.bfloat16)
        low = (factor - high.astype(jnp.float32)).astype(jnp.bfloat16)
        chosen = (wanted_ref[d] == places).astype(jnp.bfloat16)
        spread = lax.dot_general(
            chosen,
            jnp.concatenate([high, low], axis=0),
            (((1,), (1,)), ((), ())),
            preferred_element_type=jnp.float32,
        )
        depth = 4 * members
        left_ref[:, k * depth : (k + 1) * depth] = spread.astype(jnp.bfloat16)
        grads_ref, targets_ref = (
            (odd_grads_ref, odd_targets_ref) if k % 2 else (even_grads_ref, even_targets_ref)
        )
        piece = pl.ds((k // 2) * members, members)
        for twice in range(2):
            at = k * depth + twice * 2 * members
            right_ref[at : at + members, :] = grads_ref[piece, :]
            right_ref[at + members : at + 2 * members, :] = targets_ref[piece, :]
    out_ref[...] = jnp.dot(left_ref[...], right_ref[...], preferred_element_type=jnp.float32)


def on_device(rows, targets, w_up, bias, history, requests, upstream):
    score_scale = DL ** (-0.5)
    owners = lax.axis_size("batch")
    latents = lax.axis_size("latent")
    latent = lax.axis_index("latent")
    capacity = requests.shape[1]
    slot_count = owners * capacity
    members, row_width = targets.shape
    stored = rows.shape[0]
    hidden_share = upstream.shape[1]
    half = members // 2
    whole = pl.BlockSpec(memory_space=pltpu.VMEM)
    params = pltpu.CompilerParams(vmem_limit_bytes=32 * 1024 * 1024)

    wanted = exchange(requests.reshape(owners, 1, capacity))
    chosen = pl.pallas_call(
        pick_rows,
        out_shape=jax.ShapeDtypeStruct((slot_count, row_width), jnp.bfloat16),
        in_specs=[whole, whole],
        out_specs=whole,
        compiler_params=params,
        name="pick_rows",
    )(wanted, rows)
    fetched = exchange(chosen.reshape(owners, capacity, row_width)).reshape(slot_count, row_width)

    slots = lax.broadcasted_iota(jnp.int32, (1, 1, slot_count), 2)
    count = jnp.sum((history[:, :, None] == slots).astype(jnp.float32), axis=1)
    upstream_full = gather_columns(upstream, "latent")
    even_targets = gather_chips(targets, "batch")
    odd_targets = swap(even_targets, "batch", 1)
    fetched, count, upstream_full, even_targets, odd_targets = lax.optimization_barrier(
        (fetched, count, upstream_full, even_targets, odd_targets)
    )

    slot_scores = jnp.einsum("ud,sd->us", targets, fetched, preferred_element_type=jnp.float32)
    scores = sum_all(slot_scores, "latent") * score_scale
    top = jnp.max(jnp.where(count > 0, scores, -jnp.inf), axis=1, keepdims=True)
    raised = jnp.where(count > 0, count * jnp.exp(scores - top), 0.0)
    weight = raised / jnp.sum(raised, axis=1, keepdims=True)

    def pack(x):
        return (
            x.reshape(2, half, owners, capacity)
            .transpose(2, 1, 0, 3)
            .reshape(owners, half, 2 * capacity)
        )

    share = half // latents
    weight_share = lax.dynamic_slice_in_dim(pack(weight), latent * share, share, axis=1)

    pooled = jnp.dot(
        weight.astype(jnp.bfloat16), fetched, preferred_element_type=jnp.float32
    ).astype(jnp.bfloat16)
    partial_hidden = jnp.dot(pooled, w_up, preferred_element_type=jnp.float32)
    hidden = sum_all(partial_hidden.astype(jnp.bfloat16), "latent") + bias
    activated, backward = jax.vjp(jax.nn.gelu, hidden)
    output = lax.dynamic_slice_in_dim(
        activated.astype(jnp.bfloat16), latent * hidden_share, hidden_share, axis=1
    )
    slopes = backward(upstream_full.astype(jnp.float32))[0].astype(jnp.bfloat16)
    pooled_grad = jnp.einsum(
        "uh,dh->ud", slopes, w_up, preferred_element_type=jnp.float32
    ).astype(jnp.bfloat16)
    slot_slopes = jnp.einsum(
        "ud,sd->us", pooled_grad, fetched, preferred_element_type=jnp.float32
    )
    part = weight * (slot_slopes - jnp.sum(weight * slot_slopes, axis=1, keepdims=True))
    sending = jnp.concatenate([pack(part * score_scale), weight_share], axis=1)
    sent = lax.all_to_all(
        jnp.broadcast_to(sending[:, None], (owners, latents) + sending.shape[1:]).reshape(
            owners * latents, half + share, 2 * capacity
        ),
        ("batch", "latent"),
        split_axis=0,
        concat_axis=0,
        tiled=True,
    )
    even_grads = gather_chips(pooled_grad, "batch")
    odd_grads = swap(even_grads, "batch", 1)
    depth = owners * 4 * members
    row_grad = pl.pallas_call(
        functools.partial(add_rows, latents),
        out_shape=jax.ShapeDtypeStruct((stored, row_width), jnp.float32),
        in_specs=[pl.BlockSpec(memory_space=pltpu.SMEM)] + [whole] * 6,
        out_specs=whole,
        scratch_shapes=[
            pltpu.VMEM((stored, depth), jnp.bfloat16),
            pltpu.VMEM((depth, row_width), jnp.bfloat16),
        ],
        compiler_params=params,
        name="add_rows",
    )(
        lax.axis_index("batch").reshape(1).astype(jnp.int32),
        wanted,
        sent,
        even_targets,
        odd_targets,
        even_grads,
        odd_grads,
    )
    return (output, row_grad)


def solution(mesh):
    return jax.shard_map(
        on_device,
        mesh=mesh,
        in_specs=(
            P("batch", "latent"),
            P("batch", "latent"),
            P("latent", None),
            P(),
            P("batch", None),
            P("batch", None),
            P("batch", "latent"),
        ),
        out_specs=(P("batch", "latent"), P("batch", "latent")),
        check_vma=False,
    )
```

```python
import functools

import jax
import jax.numpy as jnp
from jax import lax
from jax.experimental import pallas as pl
from jax.experimental.pallas import tpu as pltpu
from jax.sharding import PartitionSpec as P

DL = 2048


def swap(x, axis, k):
    n = lax.axis_size(axis)
    return lax.ppermute(x, axis, [(i, i ^ k) for i in range(n)])


def sum_all(x, axis):
    n = lax.axis_size(axis)
    parts = [swap(x, axis, k) for k in range(1, n)]
    total = x.astype(jnp.float32)
    for part in parts:
        total = total + part.astype(jnp.float32)
    return total


def gather_columns(x, axis):
    n = lax.axis_size(axis)
    me = lax.axis_index(axis)
    parts = jnp.stack([x] + [swap(x, axis, k) for k in range(1, n)])
    ordered = [lax.dynamic_index_in_dim(parts, me ^ i, 0, keepdims=False) for i in range(n)]
    return jnp.concatenate(ordered, axis=1)


def exchange(x):
    return lax.all_to_all(x, "batch", split_axis=0, concat_axis=0, tiled=True)


def gather_chips(x, axis):
    n = lax.axis_size(axis)
    return jnp.concatenate([x] + [swap(x, axis, k) for k in range(2, n, 2)], axis=0)


def pick_rows(wanted_ref, rows_ref, out_ref, held_ref, sems):
    owners, capacity = wanted_ref.shape[0], wanted_ref.shape[2]
    stored, width = held_ref.shape
    copies = []
    for c in range(2):
        for r in range(2):
            part = (pl.ds(r * stored // 2, stored // 2), pl.ds(c * width // 2, width // 2))
            copy = pltpu.make_async_copy(rows_ref.at[part], held_ref.at[part], sems.at[c, r])
            copy.start()
            copies.append(copy)
    listed = wanted_ref[...].reshape(owners, capacity).T
    places = lax.broadcasted_iota(jnp.int32, (capacity, stored), 1)
    chosen = jnp.concatenate(
        [(listed[:, d : d + 1] == places).astype(jnp.bfloat16) for d in range(owners)], axis=0
    )
    for c in range(2):
        copies[2 * c].wait()
        copies[2 * c + 1].wait()
        columns = pl.ds(c * width // 2, width // 2)
        out_ref[:, columns] = jnp.dot(
            chosen, held_ref[:, columns], preferred_element_type=jnp.float32
        ).astype(jnp.bfloat16)


def add_rows(
    latents,
    me_ref,
    wanted_ref,
    sent_ref,
    even_ref,
    odd_ref,
    out_ref,
    left_ref,
    right_ref,
):
    owners, capacity = wanted_ref.shape[0], wanted_ref.shape[2]
    stored = out_ref.shape[0]
    members = even_ref.shape[0] // owners
    half = members // 2
    share = half // latents
    places = lax.broadcasted_iota(jnp.int32, (stored, capacity), 0)
    me = me_ref[0]

    def unpack(x):
        return jnp.concatenate([x[:, :capacity], x[:, capacity:]], axis=0)

    for k in range(owners):
        d = me ^ k
        block = sent_ref[pl.ds(d * latents, latents)]
        slope = block[0, :half]
        for z in range(1, latents):
            slope = slope + block[z, :half]
        weight = jnp.concatenate([block[z, half : half + share] for z in range(latents)], axis=0)
        factor = jnp.concatenate([unpack(weight), unpack(slope)], axis=0)
        high = factor.astype(jnp.bfloat16)
        low = (factor - high.astype(jnp.float32)).astype(jnp.bfloat16)
        chosen = (wanted_ref[d] == places).astype(jnp.bfloat16)
        spread = lax.dot_general(
            chosen,
            jnp.concatenate([high, low], axis=0),
            (((1,), (1,)), ((), ())),
            preferred_element_type=jnp.float32,
        )
        depth = 4 * members
        left_ref[:, k * depth : (k + 1) * depth] = spread.astype(jnp.bfloat16)
        side_ref = odd_ref if k % 2 else even_ref
        targets = side_ref[pl.ds((k // 2) * members, members), :]
        grads = side_ref[pl.ds((owners // 2 + k // 2) * members, members), :]
        right_ref[k * depth : (k + 1) * depth, :] = jnp.concatenate(
            [grads, targets, grads, targets], axis=0
        )
    out_ref[...] = jnp.dot(left_ref[...], right_ref[...], preferred_element_type=jnp.float32)


def on_device(rows, targets, w_up, bias, history, requests, upstream):
    score_scale = DL ** (-0.5)
    owners = lax.axis_size("batch")
    latents = lax.axis_size("latent")
    latent = lax.axis_index("latent")
    capacity = requests.shape[1]
    slot_count = owners * capacity
    members, row_width = targets.shape
    stored = rows.shape[0]
    hidden_share = upstream.shape[1]
    half = members // 2
    whole = pl.BlockSpec(memory_space=pltpu.VMEM)
    params = pltpu.CompilerParams(vmem_limit_bytes=32 * 1024 * 1024)

    wanted = exchange(requests.reshape(owners, 1, capacity))
    chosen = pl.pallas_call(
        pick_rows,
        out_shape=jax.ShapeDtypeStruct((slot_count, row_width), jnp.bfloat16),
        in_specs=[whole, pl.BlockSpec(memory_space=pltpu.HBM)],
        out_specs=whole,
        scratch_shapes=[
            pltpu.VMEM((stored, row_width), jnp.bfloat16),
            pltpu.SemaphoreType.DMA((2, 2)),
        ],
        compiler_params=pltpu.CompilerParams(vmem_limit_bytes=60 * 1024 * 1024),
        name="pick_rows",
    )(wanted, rows)

    slots = lax.broadcasted_iota(jnp.int32, (1, 1, slot_count), 2)
    count = jnp.sum((history[:, :, None] == slots).astype(jnp.float32), axis=1)
    fetched = exchange(chosen.reshape(owners, capacity, row_width)).reshape(slot_count, row_width)
    count, late_upstream = lax.optimization_barrier((count, upstream))
    upstream_full = gather_columns(late_upstream, "latent")
    fetched, count, upstream_full = lax.optimization_barrier((fetched, count, upstream_full))

    slot_scores = jnp.einsum("ud,sd->us", targets, fetched, preferred_element_type=jnp.float32)
    parts = [swap(slot_scores, "latent", k) for k in range(1, latents)]
    parts[0], late_targets = lax.optimization_barrier((parts[0], targets))
    even_targets = gather_chips(late_targets, "batch")
    scores = functools.reduce(jnp.add, parts, slot_scores) * score_scale
    top = jnp.max(jnp.where(count > 0, scores, -jnp.inf), axis=1, keepdims=True)
    raised = jnp.where(count > 0, count * jnp.exp(scores - top), 0.0)
    weight = raised / jnp.sum(raised, axis=1, keepdims=True)

    def pack(x):
        return (
            x.reshape(2, half, owners, capacity)
            .transpose(2, 1, 0, 3)
            .reshape(owners, half, 2 * capacity)
        )

    share = half // latents
    weight_share = lax.dynamic_slice_in_dim(pack(weight), latent * share, share, axis=1)

    pooled = jnp.dot(
        weight.astype(jnp.bfloat16), fetched, preferred_element_type=jnp.float32
    ).astype(jnp.bfloat16)
    partial_hidden = jnp.dot(pooled, w_up, preferred_element_type=jnp.float32)
    hidden = sum_all(partial_hidden.astype(jnp.bfloat16), "latent") + bias
    activated, backward = jax.vjp(jax.nn.gelu, hidden)
    output = lax.dynamic_slice_in_dim(
        activated.astype(jnp.bfloat16), latent * hidden_share, hidden_share, axis=1
    )
    slopes = backward(upstream_full.astype(jnp.float32))[0].astype(jnp.bfloat16)
    pooled_grad = jnp.einsum(
        "uh,dh->ud", slopes, w_up, preferred_element_type=jnp.float32
    ).astype(jnp.bfloat16)
    slot_slopes = jnp.einsum(
        "ud,sd->us", pooled_grad, fetched, preferred_element_type=jnp.float32
    )
    part = weight * (slot_slopes - jnp.sum(weight * slot_slopes, axis=1, keepdims=True))
    sending = jnp.concatenate([pack(part * score_scale), weight_share], axis=1)
    sent = lax.all_to_all(
        jnp.broadcast_to(sending[:, None], (owners, latents) + sending.shape[1:]).reshape(
            owners * latents, half + share, 2 * capacity
        ),
        ("batch", "latent"),
        split_axis=0,
        concat_axis=0,
        tiled=True,
    )
    even_grads = gather_chips(pooled_grad, "batch")
    even = jnp.concatenate([even_targets, even_grads], axis=0)
    odd = swap(even, "batch", 1)
    depth = owners * 4 * members
    row_grad = pl.pallas_call(
        functools.partial(add_rows, latents),
        out_shape=jax.ShapeDtypeStruct((stored, row_width), jnp.float32),
        in_specs=[pl.BlockSpec(memory_space=pltpu.SMEM)] + [whole] * 4,
        out_specs=whole,
        scratch_shapes=[
            pltpu.VMEM((stored, depth), jnp.bfloat16),
            pltpu.VMEM((depth, row_width), jnp.bfloat16),
        ],
        compiler_params=params,
        name="add_rows",
    )(
        lax.axis_index("batch").reshape(1).astype(jnp.int32),
        wanted,
        sent,
        even,
        odd,
    )
    return (output, row_grad)


def solution(mesh):
    return jax.shard_map(
        on_device,
        mesh=mesh,
        in_specs=(
            P("batch", "latent"),
            P("batch", "latent"),
            P("latent", None),
            P(),
            P("batch", None),
            P("batch", None),
            P("batch", "latent"),
        ),
        out_specs=(P("batch", "latent"), P("batch", "latent")),
        check_vma=False,
    )
```

```python
import functools

import jax
import jax.numpy as jnp
from jax import lax
from jax.experimental import pallas as pl
from jax.experimental.pallas import tpu as pltpu
from jax.sharding import PartitionSpec as P

DL = 2048
SCALE = DL ** (-0.5)


def swap(x, axis, k):
    n = lax.axis_size(axis)
    return lax.ppermute(x, axis, [(i, i ^ k) for i in range(n)])


def exchange(x):
    return lax.all_to_all(x, "batch", split_axis=0, concat_axis=0, tiled=True)


def call(kernel, shapes, operands, specs, scratch=()):
    return pl.pallas_call(
        kernel,
        out_shape=shapes,
        in_specs=specs,
        out_specs=jax.tree.map(lambda _: pl.BlockSpec(memory_space=pltpu.VMEM), shapes),
        scratch_shapes=list(scratch),
        compiler_params=pltpu.CompilerParams(vmem_limit_bytes=32 * 1024 * 1024),
        name=getattr(kernel, "func", kernel).__name__,
    )(*operands)


def pick_rows(wanted_ref, rows_ref, out_ref):
    owners, capacity = wanted_ref.shape[0], wanted_ref.shape[2]
    stored = rows_ref.shape[0]
    listed = wanted_ref[...].reshape(owners, capacity).T
    places = lax.broadcasted_iota(jnp.int32, (capacity, stored), 1)
    chosen = jnp.concatenate(
        [(listed[:, d : d + 1] == places).astype(jnp.bfloat16) for d in range(owners)], axis=0
    )
    out_ref[...] = jnp.dot(chosen, rows_ref[...], preferred_element_type=jnp.float32).astype(
        jnp.bfloat16
    )


def turn(owners, upstream_ref, bias_ref, w_up_ref, fetched_ref, weight_ref, *refs):
    part_refs, (activated_ref, grad_ref, sending_ref) = refs[:-3], refs[-3:]
    latents = len(part_refs)
    members, slot_count = weight_ref.shape
    capacity = slot_count // owners
    half = members // 2
    hidden = part_refs[0][...].astype(jnp.float32)
    for part_ref in part_refs[1:]:
        hidden = hidden + part_ref[...].astype(jnp.float32)
    hidden = hidden + bias_ref[...]
    activated, backward = jax.vjp(jax.nn.gelu, hidden)
    activated_ref[...] = activated.astype(jnp.bfloat16)
    slopes = backward(upstream_ref[...].astype(jnp.float32))[0].astype(jnp.bfloat16)
    along = (((1,), (1,)), ((), ()))
    grad = lax.dot_general(
        slopes, w_up_ref[...], along, preferred_element_type=jnp.float32
    ).astype(jnp.bfloat16)
    grad_ref[...] = grad
    slot_slopes = lax.dot_general(
        grad, fetched_ref[...], along, preferred_element_type=jnp.float32
    )
    weight = weight_ref[...]
    part = weight * (slot_slopes - jnp.sum(weight * slot_slopes, axis=1, keepdims=True)) * SCALE
    for o in range(owners):
        block = part[:, o * capacity : (o + 1) * capacity]
        block = jnp.concatenate([block[:half], block[half:]], axis=1)
        for z in range(latents):
            sending_ref[o * latents + z] = block


def make_late(me_ref, weight_ref, grad_ref, out_ref):
    count, _, width = out_ref.shape
    pair = (width - grad_ref.shape[1]) // 2
    for i in range(count):
        first = pl.multiple_of((me_ref[0] // 2 ^ i) * pair, pair)
        weight = weight_ref[:, pl.ds(first, pair)]
        high = weight.astype(jnp.bfloat16)
        out_ref[i, :, :pair] = high
        out_ref[i, :, pair : 2 * pair] = (weight - high.astype(jnp.float32)).astype(jnp.bfloat16)
        out_ref[i, :, 2 * pair :] = grad_ref[...]


def add_rows(latents, me_ref, wanted_ref, sent_ref, *refs):
    target_refs, late_refs, (out_ref, left_ref, right_ref) = refs[:2], refs[2:4], refs[4:]
    owners, capacity = wanted_ref.shape[0], wanted_ref.shape[2]
    stored, width = out_ref.shape
    members = late_refs[0].shape[0] // (owners // 2)
    pair = 2 * capacity
    depth = 4 * members
    places = lax.broadcasted_iota(jnp.int32, (stored, capacity), 0)
    me = me_ref[0]
    first = me % 2 == 0

    def of_me(x):
        x = x.astype(jnp.float32)
        return jnp.where(first, x[:, :capacity], x[:, capacity:]).astype(jnp.bfloat16)

    for k in range(owners):
        d = me ^ k
        block = sent_ref[pl.ds(d * latents, latents)]
        slope = block[0]
        for z in range(1, latents):
            slope = slope + block[z]
        slope = jnp.concatenate([slope[:, :capacity], slope[:, capacity:]], axis=0)
        slope_high = slope.astype(jnp.bfloat16)
        slope_low = (slope - slope_high.astype(jnp.float32)).astype(jnp.bfloat16)
        piece = slice((k // 2) * members, (k // 2 + 1) * members)
        targets = target_refs[k % 2][piece, :]
        side = late_refs[k % 2][piece, :]
        grads = side[:, 2 * pair :]
        weight_high = of_me(side[:, :pair])
        weight_low = of_me(side[:, pair : 2 * pair])
        chosen = (wanted_ref[d] == places).astype(jnp.bfloat16)
        spread = lax.dot_general(
            chosen,
            jnp.concatenate([weight_high, slope_high, weight_low, slope_low], axis=0),
            (((1,), (1,)), ((), ())),
            preferred_element_type=jnp.float32,
        )
        left_ref[:, k * depth : (k + 1) * depth] = spread.astype(jnp.bfloat16)
        right_ref[k * depth : (k + 1) * depth, :] = jnp.concatenate(
            [grads, targets, grads, targets], axis=0
        )
    out_ref[...] = jnp.dot(left_ref[...], right_ref[...], preferred_element_type=jnp.float32)


def on_device(rows, targets, w_up, bias, history, requests, upstream):
    owners = lax.axis_size("batch")
    latents = lax.axis_size("latent")
    latent = lax.axis_index("latent")
    me = lax.axis_index("batch").reshape(1).astype(jnp.int32)
    capacity = requests.shape[1]
    slot_count = owners * capacity
    members, row_width = targets.shape
    stored = rows.shape[0]
    hidden_share = upstream.shape[1]
    half = members // 2
    vmem = pl.BlockSpec(memory_space=pltpu.VMEM)
    smem = pl.BlockSpec(memory_space=pltpu.SMEM)
    shape = jax.ShapeDtypeStruct
    bf16 = jnp.bfloat16

    wanted = exchange(requests.reshape(owners, 1, capacity))
    parts = jnp.stack([upstream] + [swap(upstream, "latent", k) for k in range(1, latents)])
    upstream_full = jnp.concatenate(
        [lax.dynamic_index_in_dim(parts, latent ^ z, 0, keepdims=False) for z in range(latents)],
        axis=1,
    )
    chosen = call(
        pick_rows, shape((slot_count, row_width), bf16), (wanted, rows), [vmem, vmem]
    )

    slots = lax.broadcasted_iota(jnp.int32, (1, 1, slot_count), 2)
    count = jnp.sum((history[:, :, None] == slots).astype(jnp.float32), axis=1)
    fetched = exchange(chosen.reshape(owners, capacity, row_width)).reshape(slot_count, row_width)
    fetched, count, upstream_full = lax.optimization_barrier((fetched, count, upstream_full))

    slot_scores = jnp.einsum("ud,sd->us", targets, fetched, preferred_element_type=jnp.float32)
    parts = [slot_scores] + [swap(slot_scores, "latent", k) for k in range(1, latents)]
    parts[1], late_targets = lax.optimization_barrier((parts[1], targets))
    even_targets = [targets] + [swap(late_targets, "batch", k) for k in range(2, owners, 2)]
    scores = sum(parts[1:], parts[0]) * SCALE
    top = jnp.max(jnp.where(count > 0, scores, -jnp.inf), axis=1, keepdims=True)
    raised = jnp.where(count > 0, count * jnp.exp(scores - top), 0.0)
    weight = raised / jnp.sum(raised, axis=1, keepdims=True)

    pooled = jnp.dot(weight.astype(bf16), fetched, preferred_element_type=jnp.float32).astype(bf16)
    partial_hidden = jnp.dot(pooled, w_up, preferred_element_type=jnp.float32).astype(bf16)
    parts = [partial_hidden] + [swap(partial_hidden, "latent", k) for k in range(1, latents)]
    parts, even_targets = lax.optimization_barrier((parts, even_targets))
    even_targets = jnp.concatenate(even_targets, axis=0)
    odd_targets = swap(even_targets, "batch", 1)
    activated, pooled_grad, sending = call(
        functools.partial(turn, owners),
        (
            shape(partial_hidden.shape, bf16),
            shape((members, row_width), bf16),
            shape((owners * latents, half, 2 * capacity), jnp.float32),
        ),
        (upstream_full, bias.reshape(1, -1), w_up, fetched, weight, *parts),
        [vmem] * (5 + latents),
    )
    output = lax.dynamic_slice_in_dim(activated, latent * hidden_share, hidden_share, axis=1)

    sent = lax.all_to_all(sending, ("batch", "latent"), split_axis=0, concat_axis=0, tiled=True)
    late = call(
        make_late,
        shape((owners // 2, members, 4 * capacity + row_width), bf16),
        (me, weight, pooled_grad),
        [smem, vmem, vmem],
    )
    even_late = [late[0]] + [swap(late[k // 2], "batch", k) for k in range(2, owners, 2)]
    even_late = jnp.concatenate(even_late, axis=0)
    odd_late = swap(even_late, "batch", 1)
    depth = owners * 4 * members
    row_grad = call(
        functools.partial(add_rows, latents),
        shape((stored, row_width), jnp.float32),
        (me, wanted, sent, even_targets, odd_targets, even_late, odd_late),
        [smem] + [vmem] * 6,
        [pltpu.VMEM((stored, depth), bf16), pltpu.VMEM((depth, row_width), bf16)],
    )
    return (output, row_grad)


def solution(mesh):
    return jax.shard_map(
        on_device,
        mesh=mesh,
        in_specs=(
            P("batch", "latent"),
            P("batch", "latent"),
            P("latent", None),
            P(),
            P("batch", None),
            P("batch", None),
            P("batch", "latent"),
        ),
        out_specs=(P("batch", "latent"), P("batch", "latent")),
        check_vma=False,
    )
```

```python
import functools

import jax
import jax.numpy as jnp
from jax import lax
from jax.experimental import pallas as pl
from jax.experimental.pallas import tpu as pltpu
from jax.sharding import PartitionSpec as P

DL = 2048
SCALE = DL ** (-0.5)


def swap(x, axis, k):
    n = lax.axis_size(axis)
    return lax.ppermute(x, axis, [(i, i ^ k) for i in range(n)])


def exchange(x):
    return lax.all_to_all(x, "batch", split_axis=0, concat_axis=0, tiled=True)


def call(kernel, shapes, operands, specs, scratch=()):
    return pl.pallas_call(
        kernel,
        out_shape=shapes,
        in_specs=specs,
        out_specs=jax.tree.map(lambda _: pl.BlockSpec(memory_space=pltpu.VMEM), shapes),
        scratch_shapes=list(scratch),
        compiler_params=pltpu.CompilerParams(vmem_limit_bytes=32 * 1024 * 1024),
        name=getattr(kernel, "func", kernel).__name__,
    )(*operands)


def pick_rows(wanted_ref, rows_ref, out_ref):
    owners, capacity = wanted_ref.shape[0], wanted_ref.shape[2]
    stored = rows_ref.shape[0]
    listed = wanted_ref[...].reshape(owners, capacity).T
    places = lax.broadcasted_iota(jnp.int32, (capacity, stored), 1)
    chosen = jnp.concatenate(
        [(listed[:, d : d + 1] == places).astype(jnp.bfloat16) for d in range(owners)], axis=0
    )
    out_ref[...] = jnp.dot(chosen, rows_ref[...], preferred_element_type=jnp.float32).astype(
        jnp.bfloat16
    )


def turn(owners, upstream_ref, bias_ref, w_up_ref, fetched_ref, weight_ref, *refs):
    part_refs, (activated_ref, grad_ref, sending_ref) = refs[:-3], refs[-3:]
    latents = len(part_refs)
    members, slot_count = weight_ref.shape
    capacity = slot_count // owners
    half = members // 2
    hidden = part_refs[0][...].astype(jnp.float32)
    for part_ref in part_refs[1:]:
        hidden = hidden + part_ref[...].astype(jnp.float32)
    hidden = hidden + bias_ref[...]
    activated, backward = jax.vjp(jax.nn.gelu, hidden)
    activated_ref[...] = activated.astype(jnp.bfloat16)
    slopes = backward(upstream_ref[...].astype(jnp.float32))[0].astype(jnp.bfloat16)
    along = (((1,), (1,)), ((), ()))
    grad = lax.dot_general(
        slopes, w_up_ref[...], along, preferred_element_type=jnp.float32
    ).astype(jnp.bfloat16)
    grad_ref[...] = grad
    slot_slopes = lax.dot_general(
        grad, fetched_ref[...], along, preferred_element_type=jnp.float32
    )
    weight = weight_ref[...]
    part = weight * (slot_slopes - jnp.sum(weight * slot_slopes, axis=1, keepdims=True)) * SCALE
    for o in range(owners):
        block = part[:, o * capacity : (o + 1) * capacity]
        block = jnp.concatenate([block[:half], block[half:]], axis=1)
        for z in range(latents):
            sending_ref[o * latents + z] = block


def make_late(me_ref, weight_ref, grad_ref, out_ref):
    count, _, width = out_ref.shape
    pair = (width - grad_ref.shape[1]) // 2
    for i in range(count):
        first = pl.multiple_of((me_ref[0] // 2 ^ i) * pair, pair)
        weight = weight_ref[:, pl.ds(first, pair)]
        high = weight.astype(jnp.bfloat16)
        out_ref[i, :, :pair] = high
        out_ref[i, :, pair : 2 * pair] = (weight - high.astype(jnp.float32)).astype(jnp.bfloat16)
        out_ref[i, :, 2 * pair :] = grad_ref[...]


def add_rows(latents, me_ref, wanted_ref, sent_ref, *refs):
    target_refs, late_refs, (out_ref, left_ref, right_ref) = refs[:2], refs[2:4], refs[4:]
    owners, capacity = wanted_ref.shape[0], wanted_ref.shape[2]
    stored, width = out_ref.shape
    members = late_refs[0].shape[0] // (owners // 2)
    pair = 2 * capacity
    depth = 4 * members
    places = lax.broadcasted_iota(jnp.int32, (stored, capacity), 0)
    me = me_ref[0]
    first = me % 2 == 0

    def of_me(x):
        x = x.astype(jnp.float32)
        return jnp.where(first, x[:, :capacity], x[:, capacity:]).astype(jnp.bfloat16)

    for k in range(owners):
        d = me ^ k
        block = sent_ref[pl.ds(d * latents, latents)]
        slope = block[0]
        for z in range(1, latents):
            slope = slope + block[z]
        slope = jnp.concatenate([slope[:, :capacity], slope[:, capacity:]], axis=0)
        slope_high = slope.astype(jnp.bfloat16)
        slope_low = (slope - slope_high.astype(jnp.float32)).astype(jnp.bfloat16)
        piece = slice((k // 2) * members, (k // 2 + 1) * members)
        targets = target_refs[k % 2][piece, :]
        side = late_refs[k % 2][piece, :]
        grads = side[:, 2 * pair :]
        weight_high = of_me(side[:, :pair])
        weight_low = of_me(side[:, pair : 2 * pair])
        chosen = (wanted_ref[d] == places).astype(jnp.bfloat16)
        spread = lax.dot_general(
            chosen,
            jnp.concatenate([weight_high, slope_high, weight_low, slope_low], axis=0),
            (((1,), (1,)), ((), ())),
            preferred_element_type=jnp.float32,
        )
        left_ref[:, k * depth : (k + 1) * depth] = spread.astype(jnp.bfloat16)
        right_ref[k * depth : (k + 1) * depth, :] = jnp.concatenate(
            [grads, targets, grads, targets], axis=0
        )
    out_ref[...] = jnp.dot(left_ref[...], right_ref[...], preferred_element_type=jnp.float32)


def on_device(rows, targets, w_up, bias, history, requests, upstream):
    owners = lax.axis_size("batch")
    latents = lax.axis_size("latent")
    latent = lax.axis_index("latent")
    me = lax.axis_index("batch").reshape(1).astype(jnp.int32)
    capacity = requests.shape[1]
    slot_count = owners * capacity
    members, row_width = targets.shape
    stored = rows.shape[0]
    hidden_share = upstream.shape[1]
    half = members // 2
    vmem = pl.BlockSpec(memory_space=pltpu.VMEM)
    smem = pl.BlockSpec(memory_space=pltpu.SMEM)
    shape = jax.ShapeDtypeStruct
    bf16 = jnp.bfloat16

    wanted = exchange(requests.reshape(owners, 1, capacity))
    parts = jnp.stack([upstream] + [swap(upstream, "latent", k) for k in range(1, latents)])
    upstream_full = jnp.concatenate(
        [lax.dynamic_index_in_dim(parts, latent ^ z, 0, keepdims=False) for z in range(latents)],
        axis=1,
    )
    chosen = call(
        pick_rows, shape((slot_count, row_width), bf16), (wanted, rows), [vmem, vmem]
    )

    slots = lax.broadcasted_iota(jnp.int32, (1, 1, slot_count), 2)
    count = jnp.sum((history[:, :, None] == slots).astype(jnp.float32), axis=1)
    fetched = exchange(chosen.reshape(owners, capacity, row_width)).reshape(slot_count, row_width)
    fetched, count, upstream_full = lax.optimization_barrier((fetched, count, upstream_full))

    slot_scores = jnp.einsum("ud,sd->us", targets, fetched, preferred_element_type=jnp.float32)
    late_targets, slot_scores = lax.optimization_barrier((targets, slot_scores))
    parts = [slot_scores] + [swap(slot_scores, "latent", k) for k in range(1, latents)]
    near_targets = [swap(late_targets, "batch", k) for k in range(2, owners, 2)[:1]]
    parts, near_targets = lax.optimization_barrier((parts, near_targets))
    scores = sum(parts[1:], parts[0]) * SCALE
    top = jnp.max(jnp.where(count > 0, scores, -jnp.inf), axis=1, keepdims=True)
    raised = jnp.where(count > 0, count * jnp.exp(scores - top), 0.0)
    weight = raised / jnp.sum(raised, axis=1, keepdims=True)

    pooled = jnp.dot(weight.astype(bf16), fetched, preferred_element_type=jnp.float32).astype(bf16)
    partial_hidden = jnp.dot(pooled, w_up, preferred_element_type=jnp.float32).astype(bf16)
    partial_hidden, late_targets = lax.optimization_barrier((partial_hidden, targets))
    parts = [partial_hidden] + [swap(partial_hidden, "latent", k) for k in range(1, latents)]
    far_targets = [swap(late_targets, "batch", k) for k in range(2, owners, 2)[1:2]]
    activated, pooled_grad, sending = call(
        functools.partial(turn, owners),
        (
            shape(partial_hidden.shape, bf16),
            shape((members, row_width), bf16),
            shape((owners * latents, half, 2 * capacity), jnp.float32),
        ),
        (upstream_full, bias.reshape(1, -1), w_up, fetched, weight, *parts),
        [vmem] * (5 + latents),
    )
    output = lax.dynamic_slice_in_dim(activated, latent * hidden_share, hidden_share, axis=1)

    sending, far_targets = lax.optimization_barrier((sending, far_targets))
    sent = lax.all_to_all(sending, ("batch", "latent"), split_axis=0, concat_axis=0, tiled=True)
    late = call(
        make_late,
        shape((owners // 2, members, 4 * capacity + row_width), bf16),
        (me, weight, pooled_grad),
        [smem, vmem, vmem],
    )
    even_late = [late[0]] + [swap(late[k // 2], "batch", k) for k in range(2, owners, 2)[:2]]
    even_targets = [targets] + near_targets + far_targets
    for k in range(2, owners, 2)[2:]:
        both = swap(jnp.concatenate([late[k // 2], targets], axis=1), "batch", k)
        even_late.append(both[:, : late.shape[2]])
        even_targets.append(both[:, late.shape[2] :])
    even_late = jnp.concatenate(even_late, axis=0)
    odd_late = swap(even_late, "batch", 1)
    even_targets = jnp.concatenate(even_targets, axis=0)
    odd_targets = swap(even_targets, "batch", 1)
    depth = owners * 4 * members
    row_grad = call(
        functools.partial(add_rows, latents),
        shape((stored, row_width), jnp.float32),
        (me, wanted, sent, even_targets, odd_targets, even_late, odd_late),
        [smem] + [vmem] * 6,
        [pltpu.VMEM((stored, depth), bf16), pltpu.VMEM((depth, row_width), bf16)],
    )
    return (output, row_grad)


def solution(mesh):
    return jax.shard_map(
        on_device,
        mesh=mesh,
        in_specs=(
            P("batch", "latent"),
            P("batch", "latent"),
            P("latent", None),
            P(),
            P("batch", None),
            P("batch", None),
            P("batch", "latent"),
        ),
        out_specs=(P("batch", "latent"), P("batch", "latent")),
        check_vma=False,
    )
```

```python
import functools

import jax
import jax.numpy as jnp
from jax import lax
from jax.experimental import pallas as pl
from jax.experimental.pallas import tpu as pltpu
from jax.sharding import PartitionSpec as P

DL = 2048
SCALE = DL ** (-0.5)


def swap(x, axis, k):
    n = lax.axis_size(axis)
    return lax.ppermute(x, axis, [(i, i ^ k) for i in range(n)])


def exchange(x):
    return lax.all_to_all(x, "batch", split_axis=0, concat_axis=0, tiled=True)


def call(kernel, shapes, operands, specs, scratch=()):
    return pl.pallas_call(
        kernel,
        out_shape=shapes,
        in_specs=specs,
        out_specs=jax.tree.map(lambda _: pl.BlockSpec(memory_space=pltpu.VMEM), shapes),
        scratch_shapes=list(scratch),
        compiler_params=pltpu.CompilerParams(vmem_limit_bytes=32 * 1024 * 1024),
        name=getattr(kernel, "func", kernel).__name__,
    )(*operands)


def hold_rows(rows_ref, out_ref):
    out_ref[...] = rows_ref[...]


def pick_rows(wanted_ref, rows_ref, out_ref):
    owners, capacity = wanted_ref.shape[0], wanted_ref.shape[2]
    stored = rows_ref.shape[0]
    listed = wanted_ref[...].reshape(owners, capacity).T
    places = lax.broadcasted_iota(jnp.int32, (capacity, stored), 1)
    chosen = jnp.concatenate(
        [(listed[:, d : d + 1] == places).astype(jnp.bfloat16) for d in range(owners)], axis=0
    )
    out_ref[...] = jnp.dot(chosen, rows_ref[...], preferred_element_type=jnp.float32).astype(
        jnp.bfloat16
    )


def count_slots(history_ref, out_ref):
    members, listed = history_ref.shape
    lanes = 128
    blocks = out_ref.shape[1] // lanes
    padded = -(-blocks // 8) * 8
    block_of = lax.broadcasted_iota(jnp.int32, (padded, listed), 0)
    lane_of = lax.broadcasted_iota(jnp.int32, (lanes, listed), 0)
    history = history_ref[...]
    block, lane = jnp.right_shift(history, 7), jnp.bitwise_and(history, lanes - 1)

    def marks(x, places, users):
        return jnp.concatenate(
            [(x[u : u + 1, :] == places).astype(jnp.bfloat16) for u in users], axis=0
        )

    for first in range(0, members, 2):
        users = (first, first + 1)
        counts = lax.dot_general(
            marks(block, block_of, users),
            marks(lane, lane_of, users),
            (((1,), (1,)), ((), ())),
            preferred_element_type=jnp.float32,
        )
        for i, u in enumerate(users):
            for b in range(blocks):
                row = i * padded + b
                out_ref[u : u + 1, b * lanes : (b + 1) * lanes] = counts[
                    row : row + 1, i * lanes : (i + 1) * lanes
                ]


def turn(owners, upstream_ref, bias_ref, w_up_ref, fetched_ref, weight_ref, *refs):
    part_refs, (activated_ref, grad_ref, sending_ref) = refs[:-3], refs[-3:]
    latents = len(part_refs)
    members, slot_count = weight_ref.shape
    capacity = slot_count // owners
    half = members // 2
    hidden = part_refs[0][...].astype(jnp.float32)
    for part_ref in part_refs[1:]:
        hidden = hidden + part_ref[...].astype(jnp.float32)
    hidden = hidden + bias_ref[...]
    activated, backward = jax.vjp(jax.nn.gelu, hidden)
    activated_ref[...] = activated.astype(jnp.bfloat16)
    slopes = backward(upstream_ref[...].astype(jnp.float32))[0].astype(jnp.bfloat16)
    along = (((1,), (1,)), ((), ()))
    grad = lax.dot_general(
        slopes, w_up_ref[...], along, preferred_element_type=jnp.float32
    ).astype(jnp.bfloat16)
    grad_ref[...] = grad
    slot_slopes = lax.dot_general(
        grad, fetched_ref[...], along, preferred_element_type=jnp.float32
    )
    weight = weight_ref[...]
    part = weight * (slot_slopes - jnp.sum(weight * slot_slopes, axis=1, keepdims=True)) * SCALE
    for o in range(owners):
        block = part[:, o * capacity : (o + 1) * capacity]
        block = jnp.concatenate([block[:half], block[half:]], axis=1)
        for z in range(latents):
            sending_ref[o * latents + z] = block


def make_late(me_ref, weight_ref, grad_ref, out_ref):
    count, _, width = out_ref.shape
    pair = (width - grad_ref.shape[1]) // 2
    for i in range(count):
        first = pl.multiple_of((me_ref[0] // 2 ^ i) * pair, pair)
        weight = weight_ref[:, pl.ds(first, pair)]
        high = weight.astype(jnp.bfloat16)
        out_ref[i, :, :pair] = high
        out_ref[i, :, pair : 2 * pair] = (weight - high.astype(jnp.float32)).astype(jnp.bfloat16)
        out_ref[i, :, 2 * pair :] = grad_ref[...]


def add_rows(latents, me_ref, wanted_ref, sent_ref, *refs):
    target_refs, late_refs, (out_ref, left_ref, right_ref) = refs[:2], refs[2:4], refs[4:]
    owners, capacity = wanted_ref.shape[0], wanted_ref.shape[2]
    stored, width = out_ref.shape
    members = late_refs[0].shape[0] // (owners // 2)
    pair = 2 * capacity
    depth = 4 * members
    places = lax.broadcasted_iota(jnp.int32, (stored, capacity), 0)
    me = me_ref[0]
    first = me % 2 == 0

    def of_me(x):
        x = x.astype(jnp.float32)
        return jnp.where(first, x[:, :capacity], x[:, capacity:]).astype(jnp.bfloat16)

    for k in range(owners):
        d = me ^ k
        block = sent_ref[pl.ds(d * latents, latents)]
        slope = block[0]
        for z in range(1, latents):
            slope = slope + block[z]
        slope = jnp.concatenate([slope[:, :capacity], slope[:, capacity:]], axis=0)
        slope_high = slope.astype(jnp.bfloat16)
        slope_low = (slope - slope_high.astype(jnp.float32)).astype(jnp.bfloat16)
        piece = slice((k // 2) * members, (k // 2 + 1) * members)
        targets = target_refs[k % 2][piece, :]
        side = late_refs[k % 2][piece, :]
        grads = side[:, 2 * pair :]
        weight_high = of_me(side[:, :pair])
        weight_low = of_me(side[:, pair : 2 * pair])
        chosen = (wanted_ref[d] == places).astype(jnp.bfloat16)
        spread = lax.dot_general(
            chosen,
            jnp.concatenate([weight_high, slope_high, weight_low, slope_low], axis=0),
            (((1,), (1,)), ((), ())),
            preferred_element_type=jnp.float32,
        )
        left_ref[:, k * depth : (k + 1) * depth] = spread.astype(jnp.bfloat16)
        right_ref[k * depth : (k + 1) * depth, :] = jnp.concatenate(
            [grads, targets, grads, targets], axis=0
        )
    out_ref[...] = jnp.dot(left_ref[...], right_ref[...], preferred_element_type=jnp.float32)


def on_device(rows, targets, w_up, bias, history, requests, upstream):
    owners = lax.axis_size("batch")
    latents = lax.axis_size("latent")
    latent = lax.axis_index("latent")
    me = lax.axis_index("batch").reshape(1).astype(jnp.int32)
    capacity = requests.shape[1]
    slot_count = owners * capacity
    members, row_width = targets.shape
    stored = rows.shape[0]
    hidden_share = upstream.shape[1]
    half = members // 2
    vmem = pl.BlockSpec(memory_space=pltpu.VMEM)
    smem = pl.BlockSpec(memory_space=pltpu.SMEM)
    shape = jax.ShapeDtypeStruct
    bf16 = jnp.bfloat16

    wanted = exchange(requests.reshape(owners, 1, capacity))
    parts = jnp.stack([upstream] + [swap(upstream, "latent", k) for k in range(1, latents)])
    upstream_full = jnp.concatenate(
        [lax.dynamic_index_in_dim(parts, latent ^ z, 0, keepdims=False) for z in range(latents)],
        axis=1,
    )
    count = call(
        count_slots, shape((members, slot_count), jnp.float32), (history,), [vmem]
    )
    held = call(hold_rows, shape(rows.shape, bf16), (rows,), [vmem])
    wanted, count = lax.optimization_barrier((wanted, count))
    chosen = call(
        pick_rows, shape((slot_count, row_width), bf16), (wanted, held), [vmem, vmem]
    )

    fetched = exchange(chosen.reshape(owners, capacity, row_width)).reshape(slot_count, row_width)
    fetched, upstream_full = lax.optimization_barrier((fetched, upstream_full))

    slot_scores = jnp.einsum("ud,sd->us", targets, fetched, preferred_element_type=jnp.float32)
    late_targets, slot_scores = lax.optimization_barrier((targets, slot_scores))
    parts = [slot_scores] + [swap(slot_scores, "latent", k) for k in range(1, latents)]
    near_targets = [swap(late_targets, "batch", k) for k in range(2, owners, 2)[:1]]
    parts, near_targets = lax.optimization_barrier((parts, near_targets))
    scores = sum(parts[1:], parts[0]) * SCALE
    top = jnp.max(jnp.where(count > 0, scores, -jnp.inf), axis=1, keepdims=True)
    raised = jnp.where(count > 0, count * jnp.exp(scores - top), 0.0)
    weight = raised / jnp.sum(raised, axis=1, keepdims=True)

    pooled = jnp.dot(weight.astype(bf16), fetched, preferred_element_type=jnp.float32).astype(bf16)
    partial_hidden = jnp.dot(pooled, w_up, preferred_element_type=jnp.float32).astype(bf16)
    partial_hidden, late_targets = lax.optimization_barrier((partial_hidden, targets))
    parts = [partial_hidden] + [swap(partial_hidden, "latent", k) for k in range(1, latents)]
    far_targets = [swap(late_targets, "batch", k) for k in range(2, owners, 2)[1:2]]
    activated, pooled_grad, sending = call(
        functools.partial(turn, owners),
        (
            shape(partial_hidden.shape, bf16),
            shape((members, row_width), bf16),
            shape((owners * latents, half, 2 * capacity), jnp.float32),
        ),
        (upstream_full, bias.reshape(1, -1), w_up, fetched, weight, *parts),
        [vmem] * (5 + latents),
    )
    output = lax.dynamic_slice_in_dim(activated, latent * hidden_share, hidden_share, axis=1)

    sending, far_targets = lax.optimization_barrier((sending, far_targets))
    sent = lax.all_to_all(sending, ("batch", "latent"), split_axis=0, concat_axis=0, tiled=True)
    late = call(
        make_late,
        shape((owners // 2, members, 4 * capacity + row_width), bf16),
        (me, weight, pooled_grad),
        [smem, vmem, vmem],
    )
    even_late = [late[0]] + [swap(late[k // 2], "batch", k) for k in range(2, owners, 2)[:2]]
    even_targets = [targets] + near_targets + far_targets
    for k in range(2, owners, 2)[2:]:
        both = swap(jnp.concatenate([late[k // 2], targets], axis=1), "batch", k)
        even_late.append(both[:, : late.shape[2]])
        even_targets.append(both[:, late.shape[2] :])
    even_late = jnp.concatenate(even_late, axis=0)
    odd_late = swap(even_late, "batch", 1)
    even_targets = jnp.concatenate(even_targets, axis=0)
    odd_targets = swap(even_targets, "batch", 1)
    depth = owners * 4 * members
    row_grad = call(
        functools.partial(add_rows, latents),
        shape((stored, row_width), jnp.float32),
        (me, wanted, sent, even_targets, odd_targets, even_late, odd_late),
        [smem] + [vmem] * 6,
        [pltpu.VMEM((stored, depth), bf16), pltpu.VMEM((depth, row_width), bf16)],
    )
    return (output, row_grad)


def solution(mesh):
    return jax.shard_map(
        on_device,
        mesh=mesh,
        in_specs=(
            P("batch", "latent"),
            P("batch", "latent"),
            P("latent", None),
            P(),
            P("batch", None),
            P("batch", None),
            P("batch", "latent"),
        ),
        out_specs=(P("batch", "latent"), P("batch", "latent")),
        check_vma=False,
    )
```

```python
import functools

import jax
import jax.numpy as jnp
from jax import lax
from jax.experimental import pallas as pl
from jax.experimental.pallas import tpu as pltpu
from jax.sharding import PartitionSpec as P

DL = 2048
SCALE = DL ** (-0.5)


def swap(x, axis, k):
    n = lax.axis_size(axis)
    return lax.ppermute(x, axis, [(i, i ^ k) for i in range(n)])


def exchange(x):
    return lax.all_to_all(x, "batch", split_axis=0, concat_axis=0, tiled=True)


def call(kernel, shapes, operands, specs, scratch=()):
    return pl.pallas_call(
        kernel,
        out_shape=shapes,
        in_specs=specs,
        out_specs=jax.tree.map(lambda _: pl.BlockSpec(memory_space=pltpu.VMEM), shapes),
        scratch_shapes=list(scratch),
        compiler_params=pltpu.CompilerParams(vmem_limit_bytes=32 * 1024 * 1024),
        name=getattr(kernel, "func", kernel).__name__,
    )(*operands)


def hold_rows(rows_ref, out_ref):
    out_ref[...] = rows_ref[...]


def pick_rows(wanted_ref, rows_ref, out_ref):
    owners, capacity = wanted_ref.shape[0], wanted_ref.shape[2]
    stored = rows_ref.shape[0]
    listed = wanted_ref[...].reshape(owners, capacity).T
    places = lax.broadcasted_iota(jnp.int32, (capacity, stored), 1)
    chosen = jnp.concatenate(
        [(listed[:, d : d + 1] == places).astype(jnp.bfloat16) for d in range(owners)], axis=0
    )
    out_ref[...] = jnp.dot(chosen, rows_ref[...], preferred_element_type=jnp.float32).astype(
        jnp.bfloat16
    )


def count_slots(history_ref, out_ref):
    members, listed = history_ref.shape
    lanes = 128
    blocks = out_ref.shape[1] // lanes
    padded = -(-blocks // 8) * 8
    block_of = lax.broadcasted_iota(jnp.int32, (padded, listed), 0)
    lane_of = lax.broadcasted_iota(jnp.int32, (lanes, listed), 0)
    history = history_ref[...]
    block, lane = jnp.right_shift(history, 7), jnp.bitwise_and(history, lanes - 1)

    def marks(x, places, users):
        return jnp.concatenate(
            [(x[u : u + 1, :] == places).astype(jnp.bfloat16) for u in users], axis=0
        )

    for first in range(0, members, 2):
        users = (first, first + 1)
        counts = lax.dot_general(
            marks(block, block_of, users),
            marks(lane, lane_of, users),
            (((1,), (1,)), ((), ())),
            preferred_element_type=jnp.float32,
        )
        for i, u in enumerate(users):
            for b in range(blocks):
                row = i * padded + b
                out_ref[u : u + 1, b * lanes : (b + 1) * lanes] = counts[
                    row : row + 1, i * lanes : (i + 1) * lanes
                ]


def weigh(count_ref, fetched_ref, w_up_ref, *refs):
    part_refs, (weight_ref, hidden_ref) = refs[:-2], refs[-2:]
    scores = part_refs[0][...]
    for part_ref in part_refs[1:]:
        scores = scores + part_ref[...]
    scores = scores * SCALE
    count = count_ref[...]
    top = jnp.max(jnp.where(count > 0, scores, -jnp.inf), axis=1, keepdims=True)
    raised = jnp.where(count > 0, count * jnp.exp(scores - top), 0.0)
    weight = raised / jnp.sum(raised, axis=1, keepdims=True)
    weight_ref[...] = weight
    pooled = jnp.dot(
        weight.astype(jnp.bfloat16), fetched_ref[...], preferred_element_type=jnp.float32
    ).astype(jnp.bfloat16)
    hidden_ref[...] = jnp.dot(
        pooled, w_up_ref[...], preferred_element_type=jnp.float32
    ).astype(jnp.bfloat16)


def turn(owners, upstream_ref, bias_ref, w_up_ref, fetched_ref, weight_ref, *refs):
    part_refs, (activated_ref, grad_ref, sending_ref) = refs[:-3], refs[-3:]
    latents = len(part_refs)
    members, slot_count = weight_ref.shape
    capacity = slot_count // owners
    half = members // 2
    hidden = part_refs[0][...].astype(jnp.float32)
    for part_ref in part_refs[1:]:
        hidden = hidden + part_ref[...].astype(jnp.float32)
    hidden = hidden + bias_ref[...]
    activated, backward = jax.vjp(jax.nn.gelu, hidden)
    activated_ref[...] = activated.astype(jnp.bfloat16)
    slopes = backward(upstream_ref[...].astype(jnp.float32))[0].astype(jnp.bfloat16)
    along = (((1,), (1,)), ((), ()))
    grad = lax.dot_general(
        slopes, w_up_ref[...], along, preferred_element_type=jnp.float32
    ).astype(jnp.bfloat16)
    grad_ref[...] = grad
    slot_slopes = lax.dot_general(
        grad, fetched_ref[...], along, preferred_element_type=jnp.float32
    )
    weight = weight_ref[...]
    part = weight * (slot_slopes - jnp.sum(weight * slot_slopes, axis=1, keepdims=True)) * SCALE
    for o in range(owners):
        block = part[:, o * capacity : (o + 1) * capacity]
        block = jnp.concatenate([block[:half], block[half:]], axis=1).astype(jnp.bfloat16)
        for z in range(latents):
            sending_ref[o * latents + z] = block


def make_late(me_ref, weight_ref, grad_ref, out_ref):
    count, _, width = out_ref.shape
    pair = (width - grad_ref.shape[1]) // 2
    for i in range(count):
        first = pl.multiple_of((me_ref[0] // 2 ^ i) * pair, pair)
        weight = weight_ref[:, pl.ds(first, pair)]
        high = weight.astype(jnp.bfloat16)
        out_ref[i, :, :pair] = high
        out_ref[i, :, pair : 2 * pair] = (weight - high.astype(jnp.float32)).astype(jnp.bfloat16)
        out_ref[i, :, 2 * pair :] = grad_ref[...]


def add_rows(latents, early, me_ref, wanted_ref, sent_ref, *refs):
    target_refs, late_refs, (out_ref, left_ref, right_ref) = refs[:2], refs[2:-3], refs[-3:]
    owners, capacity = wanted_ref.shape[0], wanted_ref.shape[2]
    stored, width = out_ref.shape
    members = late_refs[0].shape[0]
    pair = 2 * capacity
    depth = 4 * members
    places = lax.broadcasted_iota(jnp.int32, (stored, capacity), 0)
    me = me_ref[0]
    first = me % 2 == 0

    def of_me(x):
        x = x.astype(jnp.float32)
        return jnp.where(first, x[:, :capacity], x[:, capacity:]).astype(jnp.bfloat16)

    for k in range(owners):
        d, i, side = me ^ k, k // 2, k % 2
        block = sent_ref[pl.ds(d * latents, latents)].astype(jnp.float32)
        slope = block[0]
        for z in range(1, latents):
            slope = slope + block[z]
        slope = jnp.concatenate([slope[:, :capacity], slope[:, capacity:]], axis=0)
        slope_high = slope.astype(jnp.bfloat16)
        slope_low = (slope - slope_high.astype(jnp.float32)).astype(jnp.bfloat16)
        late_ref = late_refs[side * (owners // 2) + i]
        grads = late_ref[:, 2 * pair : 2 * pair + width]
        if i < early:
            targets = target_refs[side][i * members : (i + 1) * members, :]
        else:
            targets = late_refs[side * (owners // 2) + (i ^ 1)][:, 2 * pair + width :]
        weight_high = of_me(late_ref[:, :pair])
        weight_low = of_me(late_ref[:, pair : 2 * pair])
        chosen = (wanted_ref[d] == places).astype(jnp.bfloat16)
        spread = lax.dot_general(
            chosen,
            jnp.concatenate([weight_high, slope_high, weight_low, slope_low], axis=0),
            (((1,), (1,)), ((), ())),
            preferred_element_type=jnp.float32,
        )
        left_ref[:, k * depth : (k + 1) * depth] = spread.astype(jnp.bfloat16)
        right_ref[k * depth : (k + 1) * depth, :] = jnp.concatenate(
            [grads, targets, grads, targets], axis=0
        )
    out_ref[...] = jnp.dot(left_ref[...], right_ref[...], preferred_element_type=jnp.float32)


def on_device(rows, targets, w_up, bias, history, requests, upstream):
    owners = lax.axis_size("batch")
    latents = lax.axis_size("latent")
    latent = lax.axis_index("latent")
    me = lax.axis_index("batch").reshape(1).astype(jnp.int32)
    capacity = requests.shape[1]
    slot_count = owners * capacity
    members, row_width = targets.shape
    stored = rows.shape[0]
    hidden_share = upstream.shape[1]
    half = members // 2
    vmem = pl.BlockSpec(memory_space=pltpu.VMEM)
    smem = pl.BlockSpec(memory_space=pltpu.SMEM)
    shape = jax.ShapeDtypeStruct
    bf16 = jnp.bfloat16

    wanted = exchange(requests.reshape(owners, 1, capacity))
    parts = jnp.stack([upstream] + [swap(upstream, "latent", k) for k in range(1, latents)])
    upstream_full = jnp.concatenate(
        [lax.dynamic_index_in_dim(parts, latent ^ z, 0, keepdims=False) for z in range(latents)],
        axis=1,
    )
    count = call(
        count_slots, shape((members, slot_count), jnp.float32), (history,), [vmem]
    )
    held = call(hold_rows, shape(rows.shape, bf16), (rows,), [vmem])
    wanted, count = lax.optimization_barrier((wanted, count))
    chosen = call(
        pick_rows, shape((slot_count, row_width), bf16), (wanted, held), [vmem, vmem]
    )

    fetched = exchange(chosen.reshape(owners, capacity, row_width)).reshape(slot_count, row_width)
    fetched, upstream_full = lax.optimization_barrier((fetched, upstream_full))

    slot_scores = jnp.einsum("ud,sd->us", targets, fetched, preferred_element_type=jnp.float32)
    late_targets, slot_scores = lax.optimization_barrier((targets, slot_scores))
    parts = [slot_scores] + [swap(slot_scores, "latent", k) for k in range(1, latents)]
    near_targets = [swap(late_targets, "batch", k) for k in range(2, owners, 2)[:1]]
    parts, near_targets = lax.optimization_barrier((parts, near_targets))
    weight, partial_hidden = call(
        weigh,
        (shape((members, slot_count), jnp.float32), shape((members, bias.shape[0]), bf16)),
        (count, fetched, w_up, *parts),
        [vmem] * (3 + latents),
    )
    partial_hidden, late_targets = lax.optimization_barrier((partial_hidden, targets))
    parts = [partial_hidden] + [swap(partial_hidden, "latent", k) for k in range(1, latents)]
    far_targets = [swap(late_targets, "batch", k) for k in range(2, owners, 2)[1:2]]
    activated, pooled_grad, sending = call(
        functools.partial(turn, owners),
        (
            shape(partial_hidden.shape, bf16),
            shape((members, row_width), bf16),
            shape((owners * latents, half, 2 * capacity), bf16),
        ),
        (upstream_full, bias.reshape(1, -1), w_up, fetched, weight, *parts),
        [vmem] * (5 + latents),
    )
    output = lax.dynamic_slice_in_dim(activated, latent * hidden_share, hidden_share, axis=1)

    sending, far_targets = lax.optimization_barrier((sending, far_targets))
    sent = lax.all_to_all(sending, ("batch", "latent"), split_axis=0, concat_axis=0, tiled=True)
    late = call(
        make_late,
        shape((owners // 2, members, 4 * capacity + row_width), bf16),
        (me, weight, pooled_grad),
        [smem, vmem, vmem],
    )
    even_targets = [targets] + near_targets + far_targets
    early = len(even_targets)
    even_late = [late[0]]
    for k in range(2, owners, 2):
        message = late[k // 2]
        if (k ^ 2) // 2 >= early:
            message = jnp.concatenate([message, near_targets[0]], axis=1)
        even_late.append(swap(message, "batch", k))
    odd_late = [swap(x, "batch", 1) for x in even_late]
    even_targets = jnp.concatenate(even_targets, axis=0)
    odd_targets = swap(even_targets, "batch", 1)
    depth = owners * 4 * members
    row_grad = call(
        functools.partial(add_rows, latents, early),
        shape((stored, row_width), jnp.float32),
        (me, wanted, sent, even_targets, odd_targets, *even_late, *odd_late),
        [smem] + [vmem] * (4 + owners),
        [pltpu.VMEM((stored, depth), bf16), pltpu.VMEM((depth, row_width), bf16)],
    )
    return (output, row_grad)


def solution(mesh):
    return jax.shard_map(
        on_device,
        mesh=mesh,
        in_specs=(
            P("batch", "latent"),
            P("batch", "latent"),
            P("latent", None),
            P(),
            P("batch", None),
            P("batch", None),
            P("batch", "latent"),
        ),
        out_specs=(P("batch", "latent"), P("batch", "latent")),
        check_vma=False,
    )
```

```python
import functools

import jax
import jax.numpy as jnp
from jax import lax
from jax.experimental import pallas as pl
from jax.experimental.pallas import tpu as pltpu
from jax.sharding import PartitionSpec as P

DL = 2048
SCALE = DL ** (-0.5)


def swap(x, axis, k):
    n = lax.axis_size(axis)
    return lax.ppermute(x, axis, [(i, i ^ k) for i in range(n)])


def exchange(x):
    return lax.all_to_all(x, "batch", split_axis=0, concat_axis=0, tiled=True)


def call(kernel, shapes, operands, specs, scratch=()):
    return pl.pallas_call(
        kernel,
        out_shape=shapes,
        in_specs=specs,
        out_specs=jax.tree.map(lambda _: pl.BlockSpec(memory_space=pltpu.VMEM), shapes),
        scratch_shapes=list(scratch),
        compiler_params=pltpu.CompilerParams(vmem_limit_bytes=32 * 1024 * 1024),
        name=getattr(kernel, "func", kernel).__name__,
    )(*operands)


def hold_rows(rows_ref, out_ref):
    out_ref[...] = rows_ref[...]


def pick_rows(wanted_ref, rows_ref, out_ref):
    owners, capacity = wanted_ref.shape[0], wanted_ref.shape[2]
    stored = rows_ref.shape[0]
    listed = wanted_ref[...].reshape(owners, capacity).T
    places = lax.broadcasted_iota(jnp.int32, (capacity, stored), 1)
    chosen = jnp.concatenate(
        [(listed[:, d : d + 1] == places).astype(jnp.bfloat16) for d in range(owners)], axis=0
    )
    out_ref[...] = jnp.dot(chosen, rows_ref[...], preferred_element_type=jnp.float32).astype(
        jnp.bfloat16
    )


def count_slots(history_ref, out_ref):
    members, listed = history_ref.shape
    lanes = 128
    blocks = out_ref.shape[1] // lanes
    padded = -(-blocks // 8) * 8
    block_of = lax.broadcasted_iota(jnp.int32, (padded, listed), 0)
    lane_of = lax.broadcasted_iota(jnp.int32, (lanes, listed), 0)
    history = history_ref[...]
    block, lane = jnp.right_shift(history, 7), jnp.bitwise_and(history, lanes - 1)

    def marks(x, places, users):
        return jnp.concatenate(
            [(x[u : u + 1, :] == places).astype(jnp.bfloat16) for u in users], axis=0
        )

    for first in range(0, members, 2):
        users = (first, first + 1)
        counts = lax.dot_general(
            marks(block, block_of, users),
            marks(lane, lane_of, users),
            (((1,), (1,)), ((), ())),
            preferred_element_type=jnp.float32,
        )
        for i, u in enumerate(users):
            for b in range(blocks):
                row = i * padded + b
                out_ref[u : u + 1, b * lanes : (b + 1) * lanes] = counts[
                    row : row + 1, i * lanes : (i + 1) * lanes
                ]


def weigh(count_ref, upstream_ref, fetched_ref, w_up_ref, *refs):
    part_refs, (weight_ref, hidden_ref) = refs[:-2], refs[-2:]
    scores = part_refs[0][...]
    for part_ref in part_refs[1:]:
        scores = scores + part_ref[...]
    scores = scores * SCALE
    count = count_ref[...]
    top = jnp.max(jnp.where(count > 0, scores, -jnp.inf), axis=1, keepdims=True)
    raised = jnp.where(count > 0, count * jnp.exp(scores - top), 0.0)
    weight = raised / jnp.sum(raised, axis=1, keepdims=True)
    weight_ref[...] = weight
    pooled = jnp.dot(
        weight.astype(jnp.bfloat16), fetched_ref[...], preferred_element_type=jnp.float32
    ).astype(jnp.bfloat16)
    units = w_up_ref.shape[1]
    hidden_ref[:, :units] = jnp.dot(
        pooled, w_up_ref[...], preferred_element_type=jnp.float32
    ).astype(jnp.bfloat16)
    hidden_ref[:, units:] = upstream_ref[...]


def turn(owners, latent_ref, bias_ref, w_up_ref, fetched_ref, weight_ref, *refs):
    part_refs, (activated_ref, grad_ref, sending_ref) = refs[:-3], refs[-3:]
    latents = len(part_refs)
    members, slot_count = weight_ref.shape
    capacity = slot_count // owners
    half = members // 2
    units = bias_ref.shape[1]
    hidden = part_refs[0][:, :units].astype(jnp.float32)
    for part_ref in part_refs[1:]:
        hidden = hidden + part_ref[:, :units].astype(jnp.float32)
    upstream = []
    for z in range(latents):
        piece = part_refs[0][:, units:].astype(jnp.float32)
        for k in range(1, latents):
            piece = jnp.where(
                latent_ref[0] ^ z == k, part_refs[k][:, units:].astype(jnp.float32), piece
            )
        upstream.append(piece)
    upstream = jnp.concatenate(upstream, axis=1)
    hidden = hidden + bias_ref[...]
    activated, backward = jax.vjp(jax.nn.gelu, hidden)
    activated_ref[...] = activated.astype(jnp.bfloat16)
    slopes = backward(upstream)[0].astype(jnp.bfloat16)
    along = (((1,), (1,)), ((), ()))
    grad = lax.dot_general(
        slopes, w_up_ref[...], along, preferred_element_type=jnp.float32
    ).astype(jnp.bfloat16)
    grad_ref[...] = grad
    slot_slopes = lax.dot_general(
        grad, fetched_ref[...], along, preferred_element_type=jnp.float32
    )
    weight = weight_ref[...]
    part = weight * (slot_slopes - jnp.sum(weight * slot_slopes, axis=1, keepdims=True)) * SCALE
    for o in range(owners):
        block = part[:, o * capacity : (o + 1) * capacity]
        block = jnp.concatenate([block[:half], block[half:]], axis=1).astype(jnp.bfloat16)
        for z in range(latents):
            sending_ref[o * latents + z] = block


def make_late(me_ref, weight_ref, grad_ref, out_ref):
    count, _, width = out_ref.shape
    pair = (width - grad_ref.shape[1]) // 2
    for i in range(count):
        first = pl.multiple_of((me_ref[0] // 2 ^ i) * pair, pair)
        weight = weight_ref[:, pl.ds(first, pair)]
        high = weight.astype(jnp.bfloat16)
        out_ref[i, :, :pair] = high
        out_ref[i, :, pair : 2 * pair] = (weight - high.astype(jnp.float32)).astype(jnp.bfloat16)
        out_ref[i, :, 2 * pair :] = grad_ref[...]


def add_rows(latents, early, me_ref, wanted_ref, sent_ref, *refs):
    target_refs, late_refs, (out_ref, left_ref, right_ref) = refs[:2], refs[2:-3], refs[-3:]
    owners, capacity = wanted_ref.shape[0], wanted_ref.shape[2]
    stored, width = out_ref.shape
    members = late_refs[0].shape[0]
    pair = 2 * capacity
    depth = 4 * members
    places = lax.broadcasted_iota(jnp.int32, (stored, capacity), 0)
    me = me_ref[0]
    first = me % 2 == 0

    def of_me(x):
        x = x.astype(jnp.float32)
        return jnp.where(first, x[:, :capacity], x[:, capacity:]).astype(jnp.bfloat16)

    for k in range(owners):
        d, i, side = me ^ k, k // 2, k % 2
        block = sent_ref[pl.ds(d * latents, latents)].astype(jnp.float32)
        slope = block[0]
        for z in range(1, latents):
            slope = slope + block[z]
        slope = jnp.concatenate([slope[:, :capacity], slope[:, capacity:]], axis=0)
        slope_high = slope.astype(jnp.bfloat16)
        slope_low = (slope - slope_high.astype(jnp.float32)).astype(jnp.bfloat16)
        late_ref = late_refs[side * (owners // 2) + i]
        grads = late_ref[:, 2 * pair : 2 * pair + width]
        if i < early:
            targets = target_refs[side][i * members : (i + 1) * members, :]
        else:
            targets = late_refs[side * (owners // 2) + (i ^ 1)][:, 2 * pair + width :]
        weight_high = of_me(late_ref[:, :pair])
        weight_low = of_me(late_ref[:, pair : 2 * pair])
        chosen = (wanted_ref[d] == places).astype(jnp.bfloat16)
        spread = lax.dot_general(
            chosen,
            jnp.concatenate([weight_high, slope_high, weight_low, slope_low], axis=0),
            (((1,), (1,)), ((), ())),
            preferred_element_type=jnp.float32,
        )
        left_ref[:, k * depth : (k + 1) * depth] = spread.astype(jnp.bfloat16)
        right_ref[k * depth : (k + 1) * depth, :] = jnp.concatenate(
            [grads, targets, grads, targets], axis=0
        )
    out_ref[...] = jnp.dot(left_ref[...], right_ref[...], preferred_element_type=jnp.float32)


def on_device(rows, targets, w_up, bias, history, requests, upstream):
    owners = lax.axis_size("batch")
    latents = lax.axis_size("latent")
    latent = lax.axis_index("latent")
    me = lax.axis_index("batch").reshape(1).astype(jnp.int32)
    capacity = requests.shape[1]
    slot_count = owners * capacity
    members, row_width = targets.shape
    stored = rows.shape[0]
    hidden_share = upstream.shape[1]
    half = members // 2
    vmem = pl.BlockSpec(memory_space=pltpu.VMEM)
    smem = pl.BlockSpec(memory_space=pltpu.SMEM)
    shape = jax.ShapeDtypeStruct
    bf16 = jnp.bfloat16

    wanted = exchange(requests.reshape(owners, 1, capacity))
    count = call(
        count_slots, shape((members, slot_count), jnp.float32), (history,), [vmem]
    )
    held = call(hold_rows, shape(rows.shape, bf16), (rows,), [vmem])
    wanted, count = lax.optimization_barrier((wanted, count))
    chosen = call(
        pick_rows, shape((slot_count, row_width), bf16), (wanted, held), [vmem, vmem]
    )

    fetched = exchange(chosen.reshape(owners, capacity, row_width)).reshape(slot_count, row_width)

    slot_scores = jnp.einsum("ud,sd->us", targets, fetched, preferred_element_type=jnp.float32)
    late_targets, slot_scores = lax.optimization_barrier((targets, slot_scores))
    parts = [slot_scores] + [swap(slot_scores, "latent", k) for k in range(1, latents)]
    near_targets = [swap(late_targets, "batch", k) for k in range(2, owners, 2)[:1]]
    parts, near_targets = lax.optimization_barrier((parts, near_targets))
    weight, partial_hidden = call(
        weigh,
        (shape((members, slot_count), jnp.float32), shape((members, bias.shape[0] + hidden_share), bf16)),
        (count, upstream, fetched, w_up, *parts),
        [vmem] * (4 + latents),
    )
    partial_hidden, late_targets = lax.optimization_barrier((partial_hidden, targets))
    parts = [partial_hidden] + [swap(partial_hidden, "latent", k) for k in range(1, latents)]
    far_targets = [swap(late_targets, "batch", k) for k in range(2, owners, 2)[1:2]]
    activated, pooled_grad, sending = call(
        functools.partial(turn, owners),
        (
            shape((members, bias.shape[0]), bf16),
            shape((members, row_width), bf16),
            shape((owners * latents, half, 2 * capacity), bf16),
        ),
        (latent.reshape(1).astype(jnp.int32), bias.reshape(1, -1), w_up, fetched, weight, *parts),
        [smem] + [vmem] * (4 + latents),
    )
    output = lax.dynamic_slice_in_dim(activated, latent * hidden_share, hidden_share, axis=1)

    sending, far_targets = lax.optimization_barrier((sending, far_targets))
    sent = lax.all_to_all(sending, ("batch", "latent"), split_axis=0, concat_axis=0, tiled=True)
    late = call(
        make_late,
        shape((owners // 2, members, 4 * capacity + row_width), bf16),
        (me, weight, pooled_grad),
        [smem, vmem, vmem],
    )
    even_targets = [targets] + near_targets + far_targets
    early = len(even_targets)
    even_late = [late[0]]
    for k in range(2, owners, 2):
        message = late[k // 2]
        if (k ^ 2) // 2 >= early:
            message = jnp.concatenate([message, near_targets[0]], axis=1)
        even_late.append(swap(message, "batch", k))
    odd_late = [swap(x, "batch", 1) for x in even_late]
    even_targets = jnp.concatenate(even_targets, axis=0)
    odd_targets = swap(even_targets, "batch", 1)
    depth = owners * 4 * members
    row_grad = call(
        functools.partial(add_rows, latents, early),
        shape((stored, row_width), jnp.float32),
        (me, wanted, sent, even_targets, odd_targets, *even_late, *odd_late),
        [smem] + [vmem] * (4 + owners),
        [pltpu.VMEM((stored, depth), bf16), pltpu.VMEM((depth, row_width), bf16)],
    )
    return (output, row_grad)


def solution(mesh):
    return jax.shard_map(
        on_device,
        mesh=mesh,
        in_specs=(
            P("batch", "latent"),
            P("batch", "latent"),
            P("latent", None),
            P(),
            P("batch", None),
            P("batch", None),
            P("batch", "latent"),
        ),
        out_specs=(P("batch", "latent"), P("batch", "latent")),
        check_vma=False,
    )
```

```python
import functools

import jax
import jax.numpy as jnp
from jax import lax
from jax.experimental import pallas as pl
from jax.experimental.pallas import tpu as pltpu
from jax.sharding import PartitionSpec as P

DL = 2048
SCALE = DL ** (-0.5)


def swap(x, axis, k):
    n = lax.axis_size(axis)
    return lax.ppermute(x, axis, [(i, i ^ k) for i in range(n)])


def exchange(x):
    return lax.all_to_all(x, "batch", split_axis=0, concat_axis=0, tiled=True)


def call(kernel, shapes, operands, specs, scratch=()):
    return pl.pallas_call(
        kernel,
        out_shape=shapes,
        in_specs=specs,
        out_specs=jax.tree.map(lambda _: pl.BlockSpec(memory_space=pltpu.VMEM), shapes),
        scratch_shapes=list(scratch),
        compiler_params=pltpu.CompilerParams(vmem_limit_bytes=32 * 1024 * 1024),
        name=getattr(kernel, "func", kernel).__name__,
    )(*operands)


def hold_rows(rows_ref, out_ref):
    out_ref[...] = rows_ref[...]


def pick_rows(wanted_ref, rows_ref, out_ref):
    owners, capacity = wanted_ref.shape[0], wanted_ref.shape[2]
    stored = rows_ref.shape[0]
    listed = wanted_ref[...].reshape(owners, capacity).T
    places = lax.broadcasted_iota(jnp.int32, (capacity, stored), 1)
    chosen = jnp.concatenate(
        [(listed[:, d : d + 1] == places).astype(jnp.bfloat16) for d in range(owners)], axis=0
    )
    out_ref[...] = jnp.dot(chosen, rows_ref[...], preferred_element_type=jnp.float32).astype(
        jnp.bfloat16
    )


def count_slots(history_ref, out_ref):
    members, listed = history_ref.shape
    lanes = 128
    blocks = out_ref.shape[1] // lanes
    padded = -(-blocks // 8) * 8
    block_of = lax.broadcasted_iota(jnp.int32, (padded, listed), 0)
    lane_of = lax.broadcasted_iota(jnp.int32, (lanes, listed), 0)
    history = history_ref[...]
    block, lane = jnp.right_shift(history, 7), jnp.bitwise_and(history, lanes - 1)

    def marks(x, places, users):
        return jnp.concatenate(
            [(x[u : u + 1, :] == places).astype(jnp.bfloat16) for u in users], axis=0
        )

    for first in range(0, members, 2):
        users = (first, first + 1)
        counts = lax.dot_general(
            marks(block, block_of, users),
            marks(lane, lane_of, users),
            (((1,), (1,)), ((), ())),
            preferred_element_type=jnp.float32,
        )
        for i, u in enumerate(users):
            for b in range(blocks):
                row = i * padded + b
                out_ref[u : u + 1, b * lanes : (b + 1) * lanes] = counts[
                    row : row + 1, i * lanes : (i + 1) * lanes
                ]


def weigh(count_ref, upstream_ref, fetched_ref, w_up_ref, *refs):
    part_refs, (weight_ref, hidden_ref) = refs[:-2], refs[-2:]
    scores = part_refs[0][...]
    for part_ref in part_refs[1:]:
        scores = scores + part_ref[...]
    scores = scores * SCALE
    count = count_ref[...]
    top = jnp.max(jnp.where(count > 0, scores, -jnp.inf), axis=1, keepdims=True)
    raised = jnp.where(count > 0, count * jnp.exp(scores - top), 0.0)
    weight = raised / jnp.sum(raised, axis=1, keepdims=True)
    weight_ref[...] = weight
    pooled = jnp.dot(
        weight.astype(jnp.bfloat16), fetched_ref[...], preferred_element_type=jnp.float32
    ).astype(jnp.bfloat16)
    units = w_up_ref.shape[1]
    hidden_ref[:, :units] = jnp.dot(
        pooled, w_up_ref[...], preferred_element_type=jnp.float32
    ).astype(jnp.bfloat16)
    hidden_ref[:, units:] = upstream_ref[...]


def turn(owners, latent_ref, bias_ref, w_up_ref, fetched_ref, weight_ref, *refs):
    part_refs, (activated_ref, grad_ref, sending_ref) = refs[:-3], refs[-3:]
    latents = len(part_refs)
    members, slot_count = weight_ref.shape
    capacity = slot_count // owners
    half = members // 2
    units = bias_ref.shape[1]
    hidden = part_refs[0][:, :units].astype(jnp.float32)
    for part_ref in part_refs[1:]:
        hidden = hidden + part_ref[:, :units].astype(jnp.float32)
    upstream = []
    for z in range(latents):
        piece = part_refs[0][:, units:].astype(jnp.float32)
        for k in range(1, latents):
            piece = jnp.where(
                latent_ref[0] ^ z == k, part_refs[k][:, units:].astype(jnp.float32), piece
            )
        upstream.append(piece)
    upstream = jnp.concatenate(upstream, axis=1)
    hidden = hidden + bias_ref[...]
    activated, backward = jax.vjp(jax.nn.gelu, hidden)
    activated_ref[...] = activated.astype(jnp.bfloat16)
    slopes = backward(upstream)[0].astype(jnp.bfloat16)
    along = (((1,), (1,)), ((), ()))
    grad = lax.dot_general(
        slopes, w_up_ref[...], along, preferred_element_type=jnp.float32
    ).astype(jnp.bfloat16)
    grad_ref[...] = grad
    slot_slopes = lax.dot_general(
        grad, fetched_ref[...], along, preferred_element_type=jnp.float32
    )
    weight = weight_ref[...]
    part = weight * (slot_slopes - jnp.sum(weight * slot_slopes, axis=1, keepdims=True)) * SCALE
    for o in range(owners):
        block = part[:, o * capacity : (o + 1) * capacity]
        block = jnp.concatenate([block[:half], block[half:]], axis=1).astype(jnp.bfloat16)
        for z in range(latents):
            sending_ref[o * latents + z] = block


def carried(k, early):
    return (k ^ 2) // 2 >= early, (k ^ 4) // 2 >= early


def make_late(early, me_ref, weight_ref, grad_ref, near_ref, far_ref, *out_refs):
    width = grad_ref.shape[1]
    pair = (out_refs[0].shape[1] - width) // 2
    half = width // 2
    for i, out_ref in enumerate(out_refs):
        first = pl.multiple_of((me_ref[0] // 2 ^ i) * pair, pair)
        weight = weight_ref[:, pl.ds(first, pair)]
        high = weight.astype(jnp.bfloat16)
        out_ref[:, :pair] = high
        out_ref[:, pair : 2 * pair] = (weight - high.astype(jnp.float32)).astype(jnp.bfloat16)
        at = 2 * pair + width
        out_ref[:, 2 * pair : at] = grad_ref[...]
        near, far = carried(2 * i, early) if i else (False, False)
        if near:
            out_ref[:, at : at + half] = near_ref[:, half:]
            at += half
        if far:
            out_ref[:, at : at + half] = far_ref[:, :half]


def add_rows(latents, early, me_ref, wanted_ref, sent_ref, *refs):
    target_refs, late_refs, (out_ref, left_ref, right_ref) = refs[:2], refs[2:-3], refs[-3:]
    owners, capacity = wanted_ref.shape[0], wanted_ref.shape[2]
    stored, width = out_ref.shape
    members = late_refs[0].shape[0]
    pair = 2 * capacity
    depth = 4 * members
    places = lax.broadcasted_iota(jnp.int32, (stored, capacity), 0)
    me = me_ref[0]
    first = me % 2 == 0

    def of_me(x):
        x = x.astype(jnp.float32)
        return jnp.where(first, x[:, :capacity], x[:, capacity:]).astype(jnp.bfloat16)

    for k in range(owners):
        d, i, side = me ^ k, k // 2, k % 2
        block = sent_ref[pl.ds(d * latents, latents)].astype(jnp.float32)
        slope = block[0]
        for z in range(1, latents):
            slope = slope + block[z]
        slope = jnp.concatenate([slope[:, :capacity], slope[:, capacity:]], axis=0)
        slope_high = slope.astype(jnp.bfloat16)
        slope_low = (slope - slope_high.astype(jnp.float32)).astype(jnp.bfloat16)
        late_ref = late_refs[side * (owners // 2) + i]
        grads = late_ref[:, 2 * pair : 2 * pair + width]
        if i < early:
            targets = target_refs[side][i * members : (i + 1) * members, :]
        else:
            half = width // 2
            base = 2 * pair + width
            near_ref = late_refs[side * (owners // 2) + (i ^ 1)]
            far_ref = late_refs[side * (owners // 2) + (i ^ 2)]
            at = base + (half if carried(2 * (i ^ 2), early)[0] else 0)
            targets = jnp.concatenate(
                [far_ref[:, at : at + half], near_ref[:, base : base + half]], axis=1
            )
        weight_high = of_me(late_ref[:, :pair])
        weight_low = of_me(late_ref[:, pair : 2 * pair])
        chosen = (wanted_ref[d] == places).astype(jnp.bfloat16)
        spread = lax.dot_general(
            chosen,
            jnp.concatenate([weight_high, slope_high, weight_low, slope_low], axis=0),
            (((1,), (1,)), ((), ())),
            preferred_element_type=jnp.float32,
        )
        left_ref[:, k * depth : (k + 1) * depth] = spread.astype(jnp.bfloat16)
        right_ref[k * depth : (k + 1) * depth, :] = jnp.concatenate(
            [grads, targets, grads, targets], axis=0
        )
    out_ref[...] = jnp.dot(left_ref[...], right_ref[...], preferred_element_type=jnp.float32)


def on_device(rows, targets, w_up, bias, history, requests, upstream):
    owners = lax.axis_size("batch")
    latents = lax.axis_size("latent")
    latent = lax.axis_index("latent")
    me = lax.axis_index("batch").reshape(1).astype(jnp.int32)
    capacity = requests.shape[1]
    slot_count = owners * capacity
    members, row_width = targets.shape
    stored = rows.shape[0]
    hidden_share = upstream.shape[1]
    half = members // 2
    vmem = pl.BlockSpec(memory_space=pltpu.VMEM)
    smem = pl.BlockSpec(memory_space=pltpu.SMEM)
    shape = jax.ShapeDtypeStruct
    bf16 = jnp.bfloat16

    wanted = exchange(requests.reshape(owners, 1, capacity))
    count = call(
        count_slots, shape((members, slot_count), jnp.float32), (history,), [vmem]
    )
    held = call(hold_rows, shape(rows.shape, bf16), (rows,), [vmem])
    wanted, count = lax.optimization_barrier((wanted, count))
    chosen = call(
        pick_rows, shape((slot_count, row_width), bf16), (wanted, held), [vmem, vmem]
    )

    fetched = exchange(chosen.reshape(owners, capacity, row_width)).reshape(slot_count, row_width)

    slot_scores = jnp.einsum("ud,sd->us", targets, fetched, preferred_element_type=jnp.float32)
    late_targets, slot_scores = lax.optimization_barrier((targets, slot_scores))
    parts = [slot_scores] + [swap(slot_scores, "latent", k) for k in range(1, latents)]
    near_targets = [swap(late_targets, "batch", k) for k in range(2, owners, 2)[:1]]
    parts, near_targets = lax.optimization_barrier((parts, near_targets))
    weight, partial_hidden = call(
        weigh,
        (shape((members, slot_count), jnp.float32), shape((members, bias.shape[0] + hidden_share), bf16)),
        (count, upstream, fetched, w_up, *parts),
        [vmem] * (4 + latents),
    )
    partial_hidden, late_targets = lax.optimization_barrier((partial_hidden, targets))
    parts = [partial_hidden] + [swap(partial_hidden, "latent", k) for k in range(1, latents)]
    far_targets = [swap(late_targets, "batch", k) for k in range(2, owners, 2)[1:2]]
    activated, pooled_grad, sending = call(
        functools.partial(turn, owners),
        (
            shape((members, bias.shape[0]), bf16),
            shape((members, row_width), bf16),
            shape((owners * latents, half, 2 * capacity), bf16),
        ),
        (latent.reshape(1).astype(jnp.int32), bias.reshape(1, -1), w_up, fetched, weight, *parts),
        [smem] + [vmem] * (4 + latents),
    )
    output = lax.dynamic_slice_in_dim(activated, latent * hidden_share, hidden_share, axis=1)

    sending, far_targets = lax.optimization_barrier((sending, far_targets))
    sent = lax.all_to_all(sending, ("batch", "latent"), split_axis=0, concat_axis=0, tiled=True)
    even_targets = [targets] + near_targets + far_targets
    early = len(even_targets)
    base = 4 * capacity + row_width
    late = call(
        functools.partial(make_late, early),
        tuple(
            shape((members, base + (sum(carried(k, early)) * row_width // 2 if k else 0)), bf16)
            for k in range(0, owners, 2)
        ),
        (me, weight, pooled_grad, near_targets[0], far_targets[0]),
        [smem] + [vmem] * 4,
    )
    even_late = [late[0]] + [swap(late[k // 2], "batch", k) for k in range(2, owners, 2)]
    odd_late = [swap(x, "batch", 1) for x in even_late]
    even_targets = jnp.concatenate(even_targets, axis=0)
    odd_targets = swap(even_targets, "batch", 1)
    depth = owners * 4 * members
    row_grad = call(
        functools.partial(add_rows, latents, early),
        shape((stored, row_width), jnp.float32),
        (me, wanted, sent, even_targets, odd_targets, *even_late, *odd_late),
        [smem] + [vmem] * (4 + owners),
        [pltpu.VMEM((stored, depth), bf16), pltpu.VMEM((depth, row_width), bf16)],
    )
    return (output, row_grad)


def solution(mesh):
    return jax.shard_map(
        on_device,
        mesh=mesh,
        in_specs=(
            P("batch", "latent"),
            P("batch", "latent"),
            P("latent", None),
            P(),
            P("batch", None),
            P("batch", None),
            P("batch", "latent"),
        ),
        out_specs=(P("batch", "latent"), P("batch", "latent")),
        check_vma=False,
    )
```
